1024 devices in a mesh: row: 8 (over x, core), col: 128 (over y, z).
Axes of the slice: x: 4, y: 4, z: 32, core: 2. Of those that a mesh axis runs over, the one named last changes fastest.
Arguments:
- rhs: bfloat16 [8, 1048576], P(None, ('row', 'col')), may hold values from -6 to 6
- points: float32 [3, 1048576], P(None, ('row', 'col')), may hold values from 0 to 128
- basis: bfloat16 [4096, 256, 64], P(('row', 'col')), may hold values from -0.375 to 0.375
- transfer: bfloat16 [4096, 64, 64], P(('row', 'col')), may hold values from -0.75 to 0.75
- leaf_coupling: bfloat16 [4096, 16, 64, 64], P(('row', 'col')), may hold values from -0.1875 to 0.1875
- coupling_list: int32 [4096, 16], P(('row', 'col')), may hold values from 0 to 4095, as said below
- coupling_count: int32 [4096], P(('row', 'col')), may hold values from 1 to 16
- coarse_coupling: bfloat16 [1024, 16, 64, 64], P(('row', 'col')), may hold values from -0.09375 to 0.09375
- coarse_list: int32 [1024, 16], P(('row', 'col')), may hold values from 0 to 1023
- coarse_count: int32 [1024], P(('row', 'col')), may hold values from 1 to 16
- owner: int32 [1024], replicated, may hold values from 0 to 1023, each once
- near_list: int32 [4096, 8], P(('row', 'col')), may hold values from 0 to 4095, as said below
- near_count: int32 [4096], P(('row', 'col')), may hold values from 1 to 8
Outputs:
- product: bfloat16 [8, 1048576], P(None, ('row', 'col'))
The draws below stay inside these ranges and needn't reach their ends.
Inputs may be any that keep to these rules, and one draw needn't show every extreme that they name: coupling_list[t, j] is a leaf whose box corner differs from t's by at most 3 in each coordinate and by 2 or 3 in at least one, each coordinate then clipped to the grid of boxes; slots at or past coupling_count[t] are padding and hold such leaves too. near_list[t, 0] is t itself; every entry is a leaf whose box touches or equals t's box, each coordinate clipped to the grid of boxes, repeats allowed; slots at or past near_count[t] are padding. `owner`: each device number appears once.
All inputs are finite; a program needn't handle non-finite values.
Results may differ from the reference program's by a relative error of at most 0.0048.
Values may be sent and summed in bfloat16 or wider, within the bound.
No kernel may reach another device: no remote copies, remote signals or barrier semaphores. Data moves between devices by JAX's collectives and lax.ppermute only.
A program may use at most 64 MiB of HBM per device.

```python
import jax
import jax.numpy as jnp
from jax import lax

LEAF = 256
K = 64
R = 8
LEAVES_DEV = 4
NCOUP = 16
NNEAR = 8
NCC = 16
LEAVES = 4096
NPTS = 1048576
N_ROW = 8
N_COL = 128
DEVICES = 1024


def leaf_corner(leaf_ids):
    device_ids = leaf_ids // LEAVES_DEV
    return (device_ids // N_COL, device_ids % N_COL, leaf_ids % LEAVES_DEV)


def leaf_number(first, second, third):
    first = jnp.clip(first, 0, N_ROW - 1)
    second = jnp.clip(second, 0, N_COL - 1)
    third = jnp.clip(third, 0, LEAVES_DEV - 1)
    return ((first * N_COL + second) * LEAVES_DEV + third).astype(jnp.int32)


def draw_points(key, part):
    key = jax.random.fold_in(key, 5)
    leaf_ids = jnp.arange(NPTS, dtype=jnp.int32) // LEAF
    first, second, third = leaf_corner(leaf_ids)
    corners = jnp.stack([first, second, third]).astype(jnp.float32)
    return corners + jax.random.uniform(key, (3, NPTS), jnp.float32)


def draw_coupling_list(key, part):
    key = jax.random.fold_in(key, 11)
    offset_key, axis_key, size_key, sign_key = jax.random.split(key, 4)
    leaf_ids = jnp.arange(LEAVES, dtype=jnp.int32)[:, None]
    first, second, third = leaf_corner(leaf_ids)
    offsets = jax.random.randint(offset_key, (3, LEAVES, NCOUP), -3, 4)
    chosen = jax.random.randint(axis_key, (LEAVES, NCOUP), 0, 3)
    reach = jax.random.randint(size_key, (LEAVES, NCOUP), 2, 4)
    signs = jax.random.randint(sign_key, (LEAVES, NCOUP), 0, 2) * 2 - 1
    axis_ids = jnp.arange(3, dtype=jnp.int32)[:, None, None]
    offsets = jnp.where(axis_ids == chosen[None], (reach * signs)[None], offsets)
    return leaf_number(first + offsets[0], second + offsets[1], third + offsets[2])


def draw_near_list(key, part):
    key = jax.random.fold_in(key, 7)
    leaf_ids = jnp.arange(LEAVES, dtype=jnp.int32)[:, None]
    first, second, third = leaf_corner(leaf_ids)
    offsets = jax.random.randint(key, (3, LEAVES, NNEAR), -1, 2)
    offsets = offsets.at[:, :, 0].set(0)
    return leaf_number(first + offsets[0], second + offsets[1], third + offsets[2])


def plant(result, rng, low, largest):
    dims = result.shape
    index_at = [jax.random.randint(jax.random.fold_in(rng, axis), (), 0, dims[axis]) for axis in range(len(dims))]
    result = result.at[tuple(index_at)].set(low)
    longest = dims.index(max(dims))
    index_at[longest] = (index_at[longest] + 1) % dims[longest]
    return result.at[tuple(index_at)].set(largest)


def levels(key, extent, cuts, low, high):
    def one(dim, blocks):
        steps = jax.random.uniform(jax.random.fold_in(jax.random.fold_in(key, 6), dim), (blocks,), jnp.float32, low / len(cuts), high / len(cuts))
        return jnp.repeat(jnp.exp(steps), extent[dim] // blocks).reshape((-1,) + (1,) * (len(extent) - dim - 1))

    loudness = one(*cuts[0])
    for cut in cuts[1:]:
        loudness = loudness * one(*cut)
    return loudness


def scatter_about(key, dims, width, limit, shards=(), kind=jnp.bfloat16):
    gain = levels(key, dims, shards, -0.22, 0.18) if shards else 1.0
    drawn = jax.random.normal(key, dims, jnp.float32) * width * gain
    return jnp.minimum(jnp.maximum(drawn, -limit), limit).astype(kind)


def setup_inputs(seed: int = 0) -> dict:
    keys = jax.random.split(jax.random.key(seed), 14)
    rhs = scatter_about(keys[0], (R, NPTS), 1.0, 6.0, ((1, 1024),))
    points = draw_points(jax.random.fold_in(keys[13], 71), 0)
    basis = scatter_about(keys[2], (LEAVES, LEAF, K), LEAF ** -0.5, 0.375, ((0, 1024),))
    transfer = scatter_about(keys[3], (LEAVES, K, K), K ** -0.5, 0.75, ((0, 1024),))
    leaf_coupling = scatter_about(keys[4], (LEAVES, NCOUP, K, K), (K * NCOUP) ** -0.5, 0.1875, ((0, 1024),))
    coupling_list = draw_coupling_list(jax.random.fold_in(keys[13], 71), 0)
    coupling_count = plant(jax.random.randint(keys[6], (LEAVES,), 1, NCOUP + 1), jax.random.fold_in(keys[6], 1), 1, NCOUP).astype(jnp.int32)
    coarse_coupling = scatter_about(keys[7], (DEVICES, NCC, K, K), (K * NCC * LEAVES_DEV) ** -0.5, 0.09375, ((0, 1024),))
    coarse_list = plant(jax.random.randint(keys[8], (DEVICES, NCC), 0, DEVICES), jax.random.fold_in(keys[8], 1), 0, DEVICES - 1).astype(jnp.int32)
    coarse_count = plant(jax.random.randint(keys[9], (DEVICES,), 1, NCC + 1), jax.random.fold_in(keys[9], 1), 1, NCC).astype(jnp.int32)
    owner = jax.random.permutation(keys[10], DEVICES).astype(jnp.int32)
    near_list = draw_near_list(jax.random.fold_in(keys[13], 71), 0)
    near_count = plant(jax.random.randint(keys[12], (LEAVES,), 1, NNEAR + 1), jax.random.fold_in(keys[12], 1), 1, NNEAR).astype(jnp.int32)
    return dict(rhs=rhs, points=points, basis=basis, transfer=transfer, leaf_coupling=leaf_coupling, coupling_list=coupling_list, coupling_count=coupling_count, coarse_coupling=coarse_coupling, coarse_list=coarse_list, coarse_count=coarse_count, owner=owner, near_list=near_list, near_count=near_count)


FOUR_PI = 12.566370614359172
SOFTEN = 0.0025

def kernel_tile(target_points, source_points):
    gap = target_points[:, :, :, None] - source_points[:, :, None, :]
    dist_sq = gap[0] * gap[0] + gap[1] * gap[1] + gap[2] * gap[2]
    return 1.0 / (FOUR_PI * jnp.sqrt(dist_sq + SOFTEN))

def reference(rhs, points, basis, transfer, leaf_coupling, coupling_list, coupling_count, coarse_coupling, coarse_list, coarse_count, owner, near_list, near_count):
    total_leaves = basis.shape[0]
    rhs_leaf = rhs.reshape(R, total_leaves, LEAF)
    point_leaf = points.reshape(3, total_leaves, LEAF)
    leaf_coeff = jnp.einsum('lpk,rlp->lrk', basis.astype(jnp.float32), rhs_leaf.astype(jnp.float32)).astype(jnp.bfloat16)
    lifted = jnp.einsum('ljk,lrj->lrk', transfer.astype(jnp.float32), leaf_coeff.astype(jnp.float32))
    cluster_coeff = lax.optimization_barrier(jnp.sum(lifted.reshape(DEVICES, LEAVES_DEV, R, K), axis=1)).astype(jnp.bfloat16)

    def device_block(device_id):
        leaf_start = (device_id * LEAVES_DEV).astype(jnp.int32)
        my_basis = lax.dynamic_slice_in_dim(basis, leaf_start, LEAVES_DEV, 0)
        my_transfer = lax.dynamic_slice_in_dim(transfer, leaf_start, LEAVES_DEV, 0)
        my_coupling = lax.dynamic_slice_in_dim(leaf_coupling, leaf_start, LEAVES_DEV, 0)
        my_list = lax.dynamic_slice_in_dim(coupling_list, leaf_start, LEAVES_DEV, 0)
        my_count = lax.dynamic_slice_in_dim(coupling_count, leaf_start, LEAVES_DEV, 0)
        my_near = lax.dynamic_slice_in_dim(near_list, leaf_start, LEAVES_DEV, 0)
        my_near_count = lax.dynamic_slice_in_dim(near_count, leaf_start, LEAVES_DEV, 0)
        my_points = lax.dynamic_slice_in_dim(point_leaf, leaf_start, LEAVES_DEV, 1)
        live_mask = jnp.arange(NCOUP)[None, :] < my_count[:, None]
        picked = jnp.where(live_mask[:, :, None, None], leaf_coeff[my_list], jnp.zeros((), jnp.bfloat16))
        far_local = jnp.einsum('tjkm,tjrm->trk', my_coupling.astype(jnp.float32), picked.astype(jnp.float32))
        coarse_live = jnp.arange(NCC) < coarse_count[device_id]
        sources = cluster_coeff[owner[coarse_list[device_id]]]
        sources = jnp.where(coarse_live[:, None, None], sources, jnp.zeros((), jnp.bfloat16))
        coarse_field = jnp.einsum('jkm,jrm->rk', coarse_coupling[device_id].astype(jnp.float32), sources.astype(jnp.float32))
        pushed = jnp.einsum('tjk,rk->trj', my_transfer.astype(jnp.float32), coarse_field, precision=lax.Precision.HIGHEST)
        local_exp = (far_local + pushed).astype(jnp.bfloat16)
        far_part = jnp.einsum('tpj,trj->rtp', my_basis.astype(jnp.float32), local_exp.astype(jnp.float32))
        near_part = jnp.zeros((R, LEAVES_DEV, LEAF), jnp.float32)
        for near_slot in range(NNEAR):
            source_ids = my_near[:, near_slot]
            tile_vals = kernel_tile(my_points, point_leaf[:, source_ids])
            tile_vals = jnp.where((near_slot < my_near_count)[:, None, None], tile_vals, jnp.float32(0.0)).astype(jnp.bfloat16)
            near_part = near_part + jnp.einsum('lpq,rlq->rlp', tile_vals.astype(jnp.float32), rhs_leaf[:, source_ids].astype(jnp.float32))
        return (near_part + far_part).astype(jnp.bfloat16)
    blocks = lax.map(device_block, jnp.arange(DEVICES, dtype=jnp.int32))
    return jnp.transpose(blocks, (1, 0, 2, 3)).reshape(R, NPTS)
```

```python
import functools

import jax
import jax.numpy as jnp
from jax import lax
from jax.experimental import pallas as pl
from jax.experimental.pallas import tpu as pltpu
from jax.sharding import Mesh, PartitionSpec as P

FOUR_PI = 12.566370614359172
SOFTEN = 0.0025
F32 = jnp.float32
BF16 = jnp.bfloat16
NT = (((1,), (1,)), ((), ()))

BLOCK = 10
SHARE = BLOCK + 2 * BLOCK + 4


def pack_kernel(rhs_ref, points_ref, basis_ref, transfer_ref, block_ref, cluster_ref):
    points = points_ref[...]
    part_hi = points.astype(BF16).astype(F32)
    rest = points - part_hi
    part_mid = rest.astype(BF16).astype(F32)
    part_lo = rest - part_mid
    parts = jnp.concatenate([part_hi, part_mid, part_lo[:2]], axis=0)
    cluster = jnp.zeros((8, 64), F32)
    coeffs = []
    last_rows = []
    for leaf in range(4):
        low = slice(leaf * 256, leaf * 256 + 128)
        high = slice(leaf * 256 + 128, leaf * 256 + 256)
        sides = rhs_ref[:, leaf * 256 : leaf * 256 + 256]
        coeff = jnp.dot(sides, basis_ref[leaf], preferred_element_type=F32).astype(BF16)
        cluster = cluster + jnp.dot(coeff, transfer_ref[leaf], preferred_element_type=F32)
        coeffs.append(coeff.astype(F32))
        wide = sides.astype(F32)
        block_ref[leaf] = jnp.concatenate([wide[:, :128], wide[:, 128:]], axis=0).astype(BF16)
        block_ref[4 + leaf] = jnp.concatenate([parts[:, low], parts[:, high]], axis=0).astype(BF16)
        last_rows += [part_lo[2:3, low], part_lo[2:3, high]]
    block_ref[8] = jnp.concatenate(last_rows + [jnp.zeros((8, 128), F32)], axis=0).astype(BF16)
    block_ref[9] = jnp.concatenate(
        [jnp.concatenate(coeffs[:2], axis=1), jnp.concatenate(coeffs[2:], axis=1)], axis=0
    ).astype(BF16)
    packed = jnp.concatenate([cluster[:4], cluster[4:]], axis=1).astype(BF16)
    cluster_ref[...] = jnp.broadcast_to(packed[None], cluster_ref.shape)


def locate(leaf_id, cols, my_col):
    device = lax.shift_right_logical(leaf_id, 2)
    row = device // cols
    gap = device - row * cols - my_col
    side = (row - lax.rem(row, 2) + jnp.where(gap < 0, 1, 0)) * SHARE
    return row, gap, side, lax.rem(leaf_id, 4)


def near_kernel(cols, pos_ref, list_ref, count_ref, points_ref, share_ref, near_ref, wide_ref):
    my_col = pos_ref[1]
    scale = F32(FOUR_PI * FOUR_PI)
    floor = F32(FOUR_PI * FOUR_PI * SOFTEN)
    row_ids = lax.broadcasted_iota(jnp.int32, (8, 128), 0)
    for leaf in range(4):
        own = points_ref[:, leaf * 256 : leaf * 256 + 256]
        own = jnp.concatenate([own, jnp.zeros((5, 256), F32)], axis=0).T
        for axis in range(3):
            wide_ref[axis] = jnp.broadcast_to(own[:, axis : axis + 1], (256, 128))

        def slot_step(slot, total):
            row, gap, side, source = locate(list_ref[leaf, slot], cols, my_col)
            base = jnp.where(gap == 0, row * SHARE, side + BLOCK + lax.rem(row, 2) * BLOCK)
            sides = share_ref[base + source].astype(F32)
            parts = share_ref[base + 4 + source].astype(F32)
            last = share_ref[base + 8].astype(F32)[:8]
            tiles = []
            for half in range(2):
                part = parts[half * 8 : half * 8 + 8]
                tail = jnp.sum(
                    jnp.where(row_ids == source * 2 + half, last, 0.0), axis=0, keepdims=True
                )
                first = wide_ref[0] - (part[0:1] + part[3:4] + part[6:7])
                second = wide_ref[1] - (part[1:2] + part[4:5] + part[7:8])
                third = wide_ref[2] - (part[2:3] + part[5:6] + tail)
                dist_sq = first * first + second * second + third * third
                tiles.append(lax.rsqrt(dist_sq * scale + floor).astype(BF16))
            tile = jnp.concatenate(tiles, axis=1)
            sides = jnp.concatenate([sides[:8], sides[8:]], axis=1).astype(BF16)
            return total + lax.dot_general(tile, sides, NT, preferred_element_type=F32)

        total = lax.fori_loop(0, count_ref[leaf], slot_step, jnp.zeros((256, 8), F32))
        near_ref[:, leaf * 256 : leaf * 256 + 256] = total.T


def couple(matrices, sources):
    slots = matrices.shape[0]
    products = lax.dot_general(
        matrices.reshape(slots * 64, 64), sources.astype(BF16), NT, preferred_element_type=F32
    )
    group = lax.broadcasted_iota(jnp.int32, (64, 128), 1) // 8
    total = jnp.zeros((64, 128), F32)
    for slot in range(slots):
        total = jnp.where(group == slot, products[slot * 64 : slot * 64 + 64], total)
    for shift in (64, 32, 16, 8):
        total = total + pltpu.roll(total, shift, 1)
    return total


def far_kernel(
    cols,
    ys,
    zs,
    pos_ref,
    coupling_list_ref,
    coupling_count_ref,
    coarse_list_ref,
    coarse_count_ref,
    owner_ref,
    share_ref,
    same_ref,
    other_ref,
    leaf_coupling_ref,
    coarse_coupling_ref,
    transfer_ref,
    basis_ref,
    near_ref,
    out_ref,
    source_ref,
):
    my_row = pos_ref[0]
    my_col = pos_ref[1]
    for slot in range(16):
        device = owner_ref[coarse_list_ref[0, slot]]
        row = device // cols
        col = device - row * cols
        tile_id = (row // 2) * (ys * zs // 4) + col // 4
        mine = lax.rem(row, 2) == lax.rem(my_row, 2)
        tile = jnp.where(mine, same_ref[tile_id], other_ref[tile_id]).astype(F32)
        place = lax.rem(col, 4)
        picked = tile[0:4]
        for step in range(1, 4):
            picked = jnp.where(place == step, tile[step * 4 : step * 4 + 4], picked)
        picked = jnp.where(slot < coarse_count_ref[0], picked, 0.0)
        source_ref[slot * 8 : slot * 8 + 8, :] = jnp.concatenate(
            [picked[:, :64], picked[:, 64:]], axis=0
        )
    coarse_field = couple(coarse_coupling_ref[0], source_ref[...])
    for leaf in range(4):
        for slot in range(16):
            row, gap, side, source = locate(coupling_list_ref[leaf, slot], cols, my_col)
            odd = lax.rem(row, 2)
            far = jnp.abs(gap)
            tile_id = jnp.where(
                far == 0,
                row * SHARE + 9,
                side + jnp.where(far == 1, 19 + odd * BLOCK, 28 + odd * 2 + far),
            )
            tile = share_ref[tile_id].astype(F32)
            half = jnp.where(source >= 2, tile[8:], tile[:8])
            half = jnp.where(lax.rem(source, 2) == 1, half[:, 64:], half[:, :64])
            live = slot < coupling_count_ref[leaf]
            source_ref[slot * 8 : slot * 8 + 8, :] = jnp.where(live, half, 0.0)
        local = couple(leaf_coupling_ref[leaf], source_ref[...])
        local = local + jnp.dot(
            transfer_ref[leaf].astype(F32),
            coarse_field,
            precision=lax.Precision.HIGHEST,
            preferred_element_type=F32,
        )
        local = local.T[:8].astype(BF16)
        far_part = lax.dot_general(local, basis_ref[leaf], NT, preferred_element_type=F32)
        span = slice(leaf * 256, leaf * 256 + 256)
        out_ref[:, span] = (near_ref[:, span] + far_part).astype(BF16)


def per_device(
    xs,
    ys,
    zs,
    rhs,
    points,
    basis,
    transfer,
    leaf_coupling,
    coupling_list,
    coupling_count,
    coarse_coupling,
    coarse_list,
    coarse_count,
    owner,
    near_list,
    near_count,
):
    cols = ys * zs
    vmem = pl.BlockSpec(memory_space=pltpu.VMEM)
    smem = pl.BlockSpec(memory_space=pltpu.SMEM)
    row_axes = ("x", "core")
    my_row = lax.axis_index(row_axes)
    my_col = lax.axis_index(("y", "z"))
    pos = jnp.stack([my_row, my_col]).astype(jnp.int32)

    block, cluster = pl.pallas_call(
        pack_kernel,
        out_shape=(
            jax.ShapeDtypeStruct((BLOCK, 16, 128), BF16),
            jax.ShapeDtypeStruct((zs, 4, 128), BF16),
        ),
        in_specs=[vmem] * 4,
        out_specs=(vmem, vmem),
        name="pack",
    )(rhs, points, basis, transfer)

    def beside(step):
        pairs = []
        for core in range(2):
            for col in range(cols):
                source = col + step if core == 0 else col - step
                if 0 <= source < cols:
                    pairs.append((core * cols + source, core * cols + col))
        return pairs

    chip = lax.all_gather(block, "core", axis=0, tiled=False)
    first = lax.ppermute(chip, ("core", "y", "z"), beside(1))
    coeffs = jnp.concatenate([chip[:, 9:], first[:, 9:]], axis=1)
    second = lax.ppermute(coeffs, ("core", "y", "z"), beside(2))
    share = jnp.concatenate(
        [block, first.reshape(2 * BLOCK, 16, 128), second.reshape(4, 16, 128)], axis=0
    )
    share, cluster = lax.optimization_barrier((share, cluster))
    shares = lax.all_gather(share, row_axes, axis=0, tiled=True)

    line = lax.all_to_all(cluster, "z", 0, 0, tiled=True).reshape(zs // 4, 16, 128)
    line = jnp.broadcast_to(line[None], (xs * ys,) + line.shape)
    same = lax.all_to_all(line, ("x", "y"), 0, 0, tiled=True).reshape(xs * cols // 4, 16, 128)
    other = lax.ppermute(same, "core", [(0, 1), (1, 0)])

    near = pl.pallas_call(
        functools.partial(near_kernel, cols),
        out_shape=jax.ShapeDtypeStruct((8, 1024), F32),
        in_specs=[smem] * 3 + [vmem] * 2,
        out_specs=vmem,
        scratch_shapes=[pltpu.VMEM((3, 256, 128), F32)],
        name="near",
        cost_estimate=pl.CostEstimate(flops=20_000_000, bytes_accessed=1_200_000, transcendentals=0),
    )(pos, near_list, near_count, points, shares)

    return pl.pallas_call(
        functools.partial(far_kernel, cols, ys, zs),
        out_shape=jax.ShapeDtypeStruct((8, 1024), BF16),
        in_specs=[smem] * 6 + [vmem] * 8,
        out_specs=vmem,
        scratch_shapes=[pltpu.VMEM((128, 64), F32)],
        name="far",
    )(
        pos,
        coupling_list,
        coupling_count,
        coarse_list,
        coarse_count,
        owner,
        shares,
        same,
        other,
        leaf_coupling,
        coarse_coupling,
        transfer,
        basis,
        near,
    )


def solution(mesh):
    rows, cols = mesh.devices.shape
    xs, ys = rows // 2, 4
    zs = cols // ys
    axes = ("x", "core", "y", "z")
    fine = Mesh(mesh.devices.reshape(xs, 2, ys, zs), axes)
    in_specs = (
        P(None, axes),
        P(None, axes),
        P(axes, None, None),
        P(axes, None, None),
        P(axes, None, None, None),
        P(axes, None),
        P(axes),
        P(axes, None, None, None),
        P(axes, None),
        P(axes),
        P(),
        P(axes, None),
        P(axes),
    )
    return jax.shard_map(
        functools.partial(per_device, xs, ys, zs),
        mesh=fine,
        in_specs=in_specs,
        out_specs=P(None, axes),
        check_vma=False,
    )
```

```python
import functools

import jax
import jax.numpy as jnp
from jax import lax
from jax.experimental import pallas as pl
from jax.experimental.pallas import tpu as pltpu
from jax.sharding import Mesh, PartitionSpec as P

FOUR_PI = 12.566370614359172
SOFTEN = 0.0025
F32 = jnp.float32
BF16 = jnp.bfloat16
NN = (((1,), (0,)), ((), ()))
NT = (((1,), (1,)), ((), ()))

BLOCK = 10


def pack_kernel(rhs_ref, points_ref, basis_ref, transfer_ref, block_ref, cluster_ref):
    points = points_ref[...]
    part_hi = points.astype(BF16).astype(F32)
    rest = points - part_hi
    part_mid = rest.astype(BF16).astype(F32)
    part_lo = rest - part_mid
    parts = jnp.concatenate([part_hi, part_mid, part_lo[:2]], axis=0)
    cluster = jnp.zeros((8, 64), F32)
    coeffs = []
    last_rows = []
    for leaf in range(4):
        low = slice(leaf * 256, leaf * 256 + 128)
        high = slice(leaf * 256 + 128, leaf * 256 + 256)
        sides = rhs_ref[:, leaf * 256 : leaf * 256 + 256]
        coeff = lax.dot_general(sides, basis_ref[leaf], NT, preferred_element_type=F32)
        coeff = coeff.astype(BF16)
        cluster = cluster + jnp.dot(coeff, transfer_ref[leaf], preferred_element_type=F32)
        coeffs.append(coeff.astype(F32))
        wide = sides.astype(F32)
        block_ref[leaf] = jnp.concatenate([wide[:, :128], wide[:, 128:]], axis=0).astype(BF16)
        block_ref[4 + leaf] = jnp.concatenate([parts[:, low], parts[:, high]], axis=0).astype(BF16)
        last_rows += [part_lo[2:3, low], part_lo[2:3, high]]
    block_ref[8] = jnp.concatenate(last_rows + [jnp.zeros((8, 128), F32)], axis=0).astype(BF16)
    block_ref[9] = jnp.concatenate(
        [jnp.concatenate(coeffs[:2], axis=1), jnp.concatenate(coeffs[2:], axis=1)], axis=0
    ).astype(BF16)
    packed = jnp.concatenate([cluster[:4], cluster[4:]], axis=1).astype(BF16)
    cluster_ref[...] = jnp.broadcast_to(packed[None], cluster_ref.shape)


def locate(leaf_id, cols):
    device = lax.shift_right_logical(leaf_id, 2)
    row = device // cols
    gap = device - row * cols - lax.axis_index(("y", "z"))
    fetched_here = (gap > 0) == (lax.axis_index("core") == 0)
    return row, gap, fetched_here, lax.rem(leaf_id, 4)


def near_kernel(
    cols,
    list_ref,
    count_ref,
    points_ref,
    own_ref,
    first_ref,
    first_mate_ref,
    near_ref,
    wide_ref,
):
    scale = F32(FOUR_PI * FOUR_PI)
    floor = F32(FOUR_PI * FOUR_PI * SOFTEN)
    row_ids = lax.broadcasted_iota(jnp.int32, (8, 128), 0)
    for leaf in range(4):
        own = points_ref[:, leaf * 256 : leaf * 256 + 256]
        own = jnp.concatenate([own, jnp.zeros((5, 256), F32)], axis=0).T
        for axis in range(3):
            wide_ref[axis] = jnp.broadcast_to(own[:, axis : axis + 1], (256, 128))

        def slot_step(slot, total):
            row, gap, here, source = locate(list_ref[leaf, slot], cols)

            def fetch(place):
                beside = jnp.where(here, first_ref[row, place], first_mate_ref[row, place])
                return jnp.where(gap == 0, own_ref[row, place], beside).astype(F32)

            sides = fetch(source)
            parts = fetch(4 + source)
            last = fetch(8)[:8]
            tiles = []
            for half in range(2):
                part = parts[half * 8 : half * 8 + 8]
                tail = jnp.sum(
                    jnp.where(row_ids == source * 2 + half, last, 0.0), axis=0, keepdims=True
                )
                first = wide_ref[0] - (part[0:1] + part[3:4] + part[6:7])
                second = wide_ref[1] - (part[1:2] + part[4:5] + part[7:8])
                third = wide_ref[2] - (part[2:3] + part[5:6] + tail)
                dist_sq = first * first + second * second + third * third
                tiles.append(lax.rsqrt(dist_sq * scale + floor).astype(BF16))
            tile = jnp.concatenate(tiles, axis=1)
            sides = jnp.concatenate([sides[:8], sides[8:]], axis=1).astype(BF16)
            return total + lax.dot_general(tile, sides, NT, preferred_element_type=F32)

        total = lax.fori_loop(0, count_ref[leaf], slot_step, jnp.zeros((256, 8), F32))
        near_ref[:, leaf * 256 : leaf * 256 + 256] = total.T


def couple(matrices, sources):
    slots = matrices.shape[0]
    products = lax.dot_general(
        matrices.reshape(slots * 64, 64), sources.astype(BF16), NT, preferred_element_type=F32
    )
    group = lax.broadcasted_iota(jnp.int32, (64, 128), 1) // 8
    total = jnp.zeros((64, 128), F32)
    for slot in range(slots):
        total = jnp.where(group == slot, products[slot * 64 : slot * 64 + 64], total)
    for shift in (64, 32, 16, 8):
        total = total + pltpu.roll(total, shift, 1)
    return total


def far_kernel(
    groups,
    cols,
    coupling_list_ref,
    coupling_count_ref,
    coarse_list_ref,
    coarse_count_ref,
    owner_ref,
    own_ref,
    first_ref,
    first_mate_ref,
    last_ref,
    last_mate_ref,
    leaf_coupling_ref,
    coarse_coupling_ref,
    transfer_ref,
    basis_ref,
    near_ref,
    out_ref,
    source_ref,
):
    my_core = lax.axis_index("core")
    for slot in range(16):
        device = owner_ref[coarse_list_ref[0, slot]]
        row = device // cols
        col = device - row * cols
        tile_id = (row // 2) * (cols // 4) + col // 4
        mine = lax.rem(row, 2) == my_core
        tile = jnp.where(mine, last_ref[tile_id], last_mate_ref[tile_id]).astype(F32)
        place = lax.rem(col, 4)
        picked = tile[0:4]
        for step in range(1, 4):
            picked = jnp.where(place == step, tile[step * 4 : step * 4 + 4], picked)
        picked = jnp.where(slot < coarse_count_ref[0], picked, 0.0)
        source_ref[slot * 8 : slot * 8 + 8, :] = jnp.concatenate(
            [picked[:, :64], picked[:, 64:]], axis=0
        )
    coarse_field = couple(coarse_coupling_ref[0], source_ref[...])
    for leaf in range(4):
        for slot in range(16):
            row, gap, here, source = locate(coupling_list_ref[leaf, slot], cols)
            far = jnp.abs(gap)
            beyond = groups + row * 2 + jnp.where(far == 3, 1, 0)
            one = jnp.where(here, first_ref[row, 9], first_mate_ref[row, 9])
            more = jnp.where(here, last_ref[beyond], last_mate_ref[beyond])
            tile = jnp.where(far == 0, own_ref[row, 9], jnp.where(far == 1, one, more))
            tile = tile.astype(F32)
            half = jnp.where(source >= 2, tile[8:], tile[:8])
            half = jnp.where(lax.rem(source, 2) == 1, half[:, 64:], half[:, :64])
            live = slot < coupling_count_ref[leaf]
            source_ref[slot * 8 : slot * 8 + 8, :] = jnp.where(live, half, 0.0)
        local = couple(leaf_coupling_ref[leaf], source_ref[...])
        local = local + jnp.dot(
            transfer_ref[leaf].astype(F32),
            coarse_field,
            precision=lax.Precision.HIGHEST,
            preferred_element_type=F32,
        )
        local = local.T[:8].astype(BF16)
        far_part = lax.dot_general(local, basis_ref[leaf], NN, preferred_element_type=F32)
        span = slice(leaf * 256, leaf * 256 + 256)
        out_ref[:, span] = (near_ref[:, span] + far_part).astype(BF16)


def per_device(
    xs,
    ys,
    zs,
    rhs,
    points,
    basis,
    transfer,
    leaf_coupling,
    coupling_list,
    coupling_count,
    coarse_coupling,
    coarse_list,
    coarse_count,
    owner,
    near_list,
    near_count,
):
    rows = 2 * xs
    cols = ys * zs
    vmem = pl.BlockSpec(memory_space=pltpu.VMEM)
    smem = pl.BlockSpec(memory_space=pltpu.SMEM)
    row_axes = ("x", "core")
    swap = [(0, 1), (1, 0)]
    groups = xs * cols // 4
    basis = jnp.swapaxes(basis, 1, 2)

    block, cluster = pl.pallas_call(
        pack_kernel,
        out_shape=(
            jax.ShapeDtypeStruct((BLOCK, 16, 128), BF16),
            jax.ShapeDtypeStruct((zs, 4, 128), BF16),
        ),
        in_specs=[vmem] * 4,
        out_specs=(vmem, vmem),
        name="pack",
    )(rhs, points, basis, transfer)

    def beside(step):
        pairs = []
        for core in range(2):
            for col in range(cols):
                source = col + step if core == 0 else col - step
                if 0 <= source < cols:
                    pairs.append((core * cols + source, core * cols + col))
        return pairs

    own = jnp.broadcast_to(block[None], (rows,) + block.shape)
    own = lax.all_to_all(own, row_axes, 0, 0, tiled=True)
    first = lax.ppermute(own, ("core", "y", "z"), beside(1))
    own, cluster = lax.optimization_barrier((own, cluster))
    line = lax.all_to_all(cluster, "z", 0, 0, tiled=True).reshape(zs // 4, 16, 128)
    first, line = lax.optimization_barrier((first, line))
    coeffs = jnp.concatenate([own[:, 9:], first[:, 9:]], axis=1)
    second = lax.ppermute(coeffs, ("core", "y", "z"), beside(2))
    first_mate = lax.ppermute(first, "core", swap)
    line = jnp.broadcast_to(line[None], (xs * ys,) + line.shape)
    line, coeffs = lax.optimization_barrier((line, coeffs))
    same = lax.all_to_all(line, ("x", "y"), 0, 0, tiled=True).reshape(groups, 16, 128)
    last = jnp.concatenate([same, second.reshape(rows * 2, 16, 128)], axis=0)
    last_mate = lax.ppermute(last, "core", swap)

    near = pl.pallas_call(
        functools.partial(near_kernel, cols),
        out_shape=jax.ShapeDtypeStruct((8, 1024), F32),
        in_specs=[smem] * 2 + [vmem] * 4,
        out_specs=vmem,
        scratch_shapes=[pltpu.VMEM((3, 256, 128), F32)],
        name="near",
        cost_estimate=pl.CostEstimate(flops=20_000_000, bytes_accessed=1_200_000, transcendentals=0),
    )(near_list, near_count, points, own, first, first_mate)

    return pl.pallas_call(
        functools.partial(far_kernel, groups, cols),
        out_shape=jax.ShapeDtypeStruct((8, 1024), BF16),
        in_specs=[smem] * 5 + [vmem] * 10,
        out_specs=vmem,
        scratch_shapes=[pltpu.VMEM((128, 64), F32)],
        name="far",
    )(
        coupling_list,
        coupling_count,
        coarse_list,
        coarse_count,
        owner,
        own,
        first,
        first_mate,
        last,
        last_mate,
        leaf_coupling,
        coarse_coupling,
        transfer,
        basis,
        near,
    )


def solution(mesh):
    rows, cols = mesh.devices.shape
    xs, ys = rows // 2, 4
    zs = cols // ys
    axes = ("x", "core", "y", "z")
    fine = Mesh(mesh.devices.reshape(xs, 2, ys, zs), axes)
    in_specs = (
        P(None, axes),
        P(None, axes),
        P(axes, None, None),
        P(axes, None, None),
        P(axes, None, None, None),
        P(axes, None),
        P(axes),
        P(axes, None, None, None),
        P(axes, None),
        P(axes),
        P(),
        P(axes, None),
        P(axes),
    )
    return jax.shard_map(
        functools.partial(per_device, xs, ys, zs),
        mesh=fine,
        in_specs=in_specs,
        out_specs=P(None, axes),
        check_vma=False,
    )
```

```python
import functools

import jax
import jax.numpy as jnp
from jax import lax
from jax.experimental import pallas as pl
from jax.experimental.pallas import tpu as pltpu
from jax.sharding import Mesh, PartitionSpec as P

FOUR_PI = 12.566370614359172
SOFTEN = 0.0025
F32 = jnp.float32
BF16 = jnp.bfloat16
NN = (((1,), (0,)), ((), ()))
NT = (((1,), (1,)), ((), ()))

BLOCK = 10


def pack_kernel(rhs_ref, points_ref, basis_ref, transfer_ref, block_ref, cluster_ref):
    points = points_ref[...]
    part_hi = points.astype(BF16).astype(F32)
    rest = points - part_hi
    part_mid = rest.astype(BF16).astype(F32)
    part_lo = rest - part_mid
    parts = jnp.concatenate([part_hi, part_mid, part_lo[:2]], axis=0)
    cluster = jnp.zeros((8, 64), F32)
    coeffs = []
    last_rows = []
    for leaf in range(4):
        low = slice(leaf * 256, leaf * 256 + 128)
        high = slice(leaf * 256 + 128, leaf * 256 + 256)
        sides = rhs_ref[:, leaf * 256 : leaf * 256 + 256]
        coeff = lax.dot_general(sides, basis_ref[leaf], NT, preferred_element_type=F32)
        coeff = coeff.astype(BF16)
        cluster = cluster + jnp.dot(coeff, transfer_ref[leaf], preferred_element_type=F32)
        coeffs.append(coeff.astype(F32))
        wide = sides.astype(F32)
        block_ref[leaf] = jnp.concatenate([wide[:, :128], wide[:, 128:]], axis=0).astype(BF16)
        block_ref[4 + leaf] = jnp.concatenate([parts[:, low], parts[:, high]], axis=0).astype(BF16)
        last_rows += [part_lo[2:3, low], part_lo[2:3, high]]
    block_ref[8] = jnp.concatenate(last_rows + [jnp.zeros((8, 128), F32)], axis=0).astype(BF16)
    block_ref[9] = jnp.concatenate(
        [jnp.concatenate(coeffs[:2], axis=1), jnp.concatenate(coeffs[2:], axis=1)], axis=0
    ).astype(BF16)
    packed = jnp.concatenate([cluster[:4], cluster[4:]], axis=1).astype(BF16)
    cluster_ref[...] = jnp.broadcast_to(packed[None], cluster_ref.shape)


def locate(leaf_id, cols):
    device = lax.shift_right_logical(leaf_id, 2)
    row = device // cols
    gap = device - row * cols - lax.axis_index(("y", "z"))
    fetched_here = (gap > 0) == (lax.axis_index("core") == 0)
    return row, gap, fetched_here, lax.rem(leaf_id, 4)


def near_kernel(
    cols,
    list_ref,
    count_ref,
    points_ref,
    own_ref,
    first_ref,
    first_mate_ref,
    near_ref,
    wide_ref,
):
    scale = F32(FOUR_PI * FOUR_PI)
    floor = F32(FOUR_PI * FOUR_PI * SOFTEN)
    row_ids = lax.broadcasted_iota(jnp.int32, (8, 128), 0)
    for leaf in range(4):
        own = points_ref[:, leaf * 256 : leaf * 256 + 256]
        own = jnp.concatenate([own, jnp.zeros((5, 256), F32)], axis=0).T
        for axis in range(3):
            wide_ref[axis] = jnp.broadcast_to(own[:, axis : axis + 1], (256, 128))

        def slot_step(slot, total):
            row, gap, here, source = locate(list_ref[leaf, slot], cols)

            def fetch(place):
                beside = jnp.where(here, first_ref[row, place], first_mate_ref[row, place])
                return jnp.where(gap == 0, own_ref[row, place], beside).astype(F32)

            sides = fetch(source)
            parts = fetch(4 + source)
            last = fetch(8)[:8]
            tiles = []
            for half in range(2):
                part = parts[half * 8 : half * 8 + 8]
                tail = jnp.sum(
                    jnp.where(row_ids == source * 2 + half, last, 0.0), axis=0, keepdims=True
                )
                first = wide_ref[0] - (part[0:1] + part[3:4] + part[6:7])
                second = wide_ref[1] - (part[1:2] + part[4:5] + part[7:8])
                third = wide_ref[2] - (part[2:3] + part[5:6] + tail)
                dist_sq = first * first + second * second + third * third
                tiles.append(lax.rsqrt(dist_sq * scale + floor).astype(BF16))
            tile = jnp.concatenate(tiles, axis=1)
            sides = jnp.concatenate([sides[:8], sides[8:]], axis=1).astype(BF16)
            return total + lax.dot_general(tile, sides, NT, preferred_element_type=F32)

        total = lax.fori_loop(0, count_ref[leaf], slot_step, jnp.zeros((256, 8), F32))
        near_ref[:, leaf * 256 : leaf * 256 + 256] = total.T


def couple(matrices, sources):
    slots = matrices.shape[0]
    products = lax.dot_general(
        matrices.reshape(slots * 64, 64), sources.astype(BF16), NT, preferred_element_type=F32
    )
    group = lax.broadcasted_iota(jnp.int32, (64, 128), 1) // 8
    total = jnp.zeros((64, 128), F32)
    for slot in range(slots):
        total = jnp.where(group == slot, products[slot * 64 : slot * 64 + 64], total)
    for shift in (64, 32, 16, 8):
        total = total + pltpu.roll(total, shift, 1)
    return total


def far_kernel(
    groups,
    cols,
    zs,
    coupling_list_ref,
    coupling_count_ref,
    coarse_list_ref,
    coarse_count_ref,
    owner_ref,
    own_ref,
    first_ref,
    first_mate_ref,
    last_ref,
    last_mate_ref,
    leaf_coupling_ref,
    coarse_coupling_ref,
    transfer_ref,
    basis_ref,
    near_ref,
    out_ref,
    source_ref,
):
    my_core = lax.axis_index("core")
    for slot in range(16):
        device = owner_ref[coarse_list_ref[0, slot]]
        row = device // cols
        col = device - row * cols
        col = col - lax.rem(col, zs) + lax.rem(col + zs // 2, zs)
        tile_id = (row // 2) * (cols // 4) + col // 4
        mine = lax.rem(row, 2) == my_core
        tile = jnp.where(mine, last_ref[tile_id], last_mate_ref[tile_id]).astype(F32)
        place = lax.rem(col, 4)
        picked = tile[0:4]
        for step in range(1, 4):
            picked = jnp.where(place == step, tile[step * 4 : step * 4 + 4], picked)
        picked = jnp.where(slot < coarse_count_ref[0], picked, 0.0)
        source_ref[slot * 8 : slot * 8 + 8, :] = jnp.concatenate(
            [picked[:, :64], picked[:, 64:]], axis=0
        )
    coarse_field = couple(coarse_coupling_ref[0], source_ref[...])
    for leaf in range(4):
        for slot in range(16):
            row, gap, here, source = locate(coupling_list_ref[leaf, slot], cols)
            far = jnp.abs(gap)
            beyond = groups + row * 2 + jnp.where(far == 3, 1, 0)
            one = jnp.where(here, first_ref[row, 9], first_mate_ref[row, 9])
            more = jnp.where(here, last_ref[beyond], last_mate_ref[beyond])
            tile = jnp.where(far == 0, own_ref[row, 9], jnp.where(far == 1, one, more))
            tile = tile.astype(F32)
            half = jnp.where(source >= 2, tile[8:], tile[:8])
            half = jnp.where(lax.rem(source, 2) == 1, half[:, 64:], half[:, :64])
            live = slot < coupling_count_ref[leaf]
            source_ref[slot * 8 : slot * 8 + 8, :] = jnp.where(live, half, 0.0)
        local = couple(leaf_coupling_ref[leaf], source_ref[...])
        local = local + jnp.dot(
            transfer_ref[leaf].astype(F32),
            coarse_field,
            precision=lax.Precision.HIGHEST,
            preferred_element_type=F32,
        )
        local = local.T[:8].astype(BF16)
        far_part = lax.dot_general(local, basis_ref[leaf], NN, preferred_element_type=F32)
        span = slice(leaf * 256, leaf * 256 + 256)
        out_ref[:, span] = (near_ref[:, span] + far_part).astype(BF16)


def per_device(
    xs,
    ys,
    zs,
    rhs,
    points,
    basis,
    transfer,
    leaf_coupling,
    coupling_list,
    coupling_count,
    coarse_coupling,
    coarse_list,
    coarse_count,
    owner,
    near_list,
    near_count,
):
    rows = 2 * xs
    cols = ys * zs
    vmem = pl.BlockSpec(memory_space=pltpu.VMEM)
    smem = pl.BlockSpec(memory_space=pltpu.SMEM)
    row_axes = ("x", "core")
    swap = [(0, 1), (1, 0)]
    groups = xs * cols // 4
    turned = [(place + zs // 2) % zs for place in range(zs)]
    basis = jnp.swapaxes(basis, 1, 2)

    block, cluster = pl.pallas_call(
        pack_kernel,
        out_shape=(
            jax.ShapeDtypeStruct((BLOCK, 16, 128), BF16),
            jax.ShapeDtypeStruct((zs, 4, 128), BF16),
        ),
        in_specs=[vmem] * 4,
        out_specs=(vmem, vmem),
        name="pack",
    )(rhs, points, basis, transfer)

    def beside(step):
        pairs = []
        for core in range(2):
            for col in range(cols):
                source = col + step if core == 0 else col - step
                if 0 <= source < cols:
                    pairs.append((core * cols + source, core * cols + col))
        return pairs

    own = jnp.broadcast_to(block[None], (rows,) + block.shape)
    own = lax.all_to_all(own, row_axes, 0, 0, tiled=True)
    first = lax.ppermute(own, ("core", "y", "z"), beside(1))
    own, cluster = lax.optimization_barrier((own, cluster))
    line = lax.all_to_all(
        cluster, "z", 0, 0, tiled=True, axis_index_groups=[turned]
    ).reshape(zs // 4, 16, 128)
    first, line = lax.optimization_barrier((first, line))
    first_mate = lax.ppermute(first, "core", swap)
    coeffs = jnp.concatenate([own[:, 9:], first[:, 9:]], axis=1)
    second = lax.ppermute(coeffs, ("core", "y", "z"), beside(2))
    line = jnp.broadcast_to(line[None], (xs * ys,) + line.shape)
    same = lax.all_to_all(line, ("x", "y"), 0, 0, tiled=True).reshape(groups, 16, 128)

    near = pl.pallas_call(
        functools.partial(near_kernel, cols),
        out_shape=jax.ShapeDtypeStruct((8, 1024), F32),
        in_specs=[smem] * 2 + [vmem] * 4,
        out_specs=vmem,
        scratch_shapes=[pltpu.VMEM((3, 256, 128), F32)],
        name="near",
        cost_estimate=pl.CostEstimate(
            flops=4_000_000_000, bytes_accessed=1_200_000, transcendentals=0
        ),
    )(near_list, near_count, points, own, first, first_mate)

    same, second, near = lax.optimization_barrier((same, second, near))
    last = jnp.concatenate([same, second.reshape(rows * 2, 16, 128)], axis=0)
    last_mate = lax.ppermute(last, "core", swap)

    return pl.pallas_call(
        functools.partial(far_kernel, groups, cols, zs),
        out_shape=jax.ShapeDtypeStruct((8, 1024), BF16),
        in_specs=[smem] * 5 + [vmem] * 10,
        out_specs=vmem,
        scratch_shapes=[pltpu.VMEM((128, 64), F32)],
        name="far",
    )(
        coupling_list,
        coupling_count,
        coarse_list,
        coarse_count,
        owner,
        own,
        first,
        first_mate,
        last,
        last_mate,
        leaf_coupling,
        coarse_coupling,
        transfer,
        basis,
        near,
    )


def solution(mesh):
    rows, cols = mesh.devices.shape
    xs, ys = rows // 2, 4
    zs = cols // ys
    axes = ("x", "core", "y", "z")
    fine = Mesh(mesh.devices.reshape(xs, 2, ys, zs), axes)
    in_specs = (
        P(None, axes),
        P(None, axes),
        P(axes, None, None),
        P(axes, None, None),
        P(axes, None, None, None),
        P(axes, None),
        P(axes),
        P(axes, None, None, None),
        P(axes, None),
        P(axes),
        P(),
        P(axes, None),
        P(axes),
    )
    return jax.shard_map(
        functools.partial(per_device, xs, ys, zs),
        mesh=fine,
        in_specs=in_specs,
        out_specs=P(None, axes),
        check_vma=False,
    )
```

```python
import functools

import jax
import jax.numpy as jnp
from jax import lax
from jax.experimental import pallas as pl
from jax.experimental.pallas import tpu as pltpu
from jax.sharding import Mesh, PartitionSpec as P

FOUR_PI = 12.566370614359172
SOFTEN = 0.0025
F32 = jnp.float32
BF16 = jnp.bfloat16
NN = (((1,), (0,)), ((), ()))
NT = (((1,), (1,)), ((), ()))

BLOCK = 10


def pack_kernel(rhs_ref, points_ref, basis_ref, transfer_ref, copies_ref, cluster_ref):
    block_ref = copies_ref.at[0]
    points = points_ref[...]
    part_hi = points.astype(BF16).astype(F32)
    rest = points - part_hi
    part_mid = rest.astype(BF16).astype(F32)
    part_lo = rest - part_mid
    parts = jnp.concatenate([part_hi, part_mid, part_lo[:2]], axis=0)
    cluster = jnp.zeros((8, 64), F32)
    coeffs = []
    last_rows = []
    for leaf in range(4):
        low = slice(leaf * 256, leaf * 256 + 128)
        high = slice(leaf * 256 + 128, leaf * 256 + 256)
        sides = rhs_ref[:, leaf * 256 : leaf * 256 + 256]
        coeff = lax.dot_general(sides, basis_ref[leaf], NT, preferred_element_type=F32)
        coeff = coeff.astype(BF16)
        cluster = cluster + jnp.dot(coeff, transfer_ref[leaf], preferred_element_type=F32)
        coeffs.append(coeff.astype(F32))
        wide = sides.astype(F32)
        block_ref[leaf] = jnp.concatenate([wide[:, :128], wide[:, 128:]], axis=0).astype(BF16)
        block_ref[4 + leaf] = jnp.concatenate([parts[:, low], parts[:, high]], axis=0).astype(BF16)
        last_rows += [part_lo[2:3, low], part_lo[2:3, high]]
    block_ref[8] = jnp.concatenate(last_rows + [jnp.zeros((8, 128), F32)], axis=0).astype(BF16)
    block_ref[9] = jnp.concatenate(
        [jnp.concatenate(coeffs[:2], axis=1), jnp.concatenate(coeffs[2:], axis=1)], axis=0
    ).astype(BF16)
    block = block_ref[...]
    for copy in range(1, copies_ref.shape[0]):
        copies_ref[copy] = block
    packed = jnp.concatenate([cluster[:4], cluster[4:]], axis=1).astype(BF16)
    cluster_ref[...] = jnp.broadcast_to(packed[None], cluster_ref.shape)


def locate(leaf_id, cols):
    device = lax.shift_right_logical(leaf_id, 2)
    row = lax.shift_right_logical(device, cols.bit_length() - 1)
    gap = (device & (cols - 1)) - lax.axis_index(("y", "z"))
    fetched_here = (gap > 0) == (lax.axis_index("core") == 0)
    return row, gap, fetched_here, leaf_id & 3


def near_kernel(
    cols,
    list_ref,
    count_ref,
    points_ref,
    own_ref,
    first_ref,
    first_mate_ref,
    near_ref,
    wide_ref,
):
    scale = F32(FOUR_PI * FOUR_PI)
    floor = F32(FOUR_PI * FOUR_PI * SOFTEN)
    row_ids = lax.broadcasted_iota(jnp.int32, (8, 128), 0)

    def source_of(leaf, slot):
        row, gap, here, source = locate(list_ref[leaf, slot], cols)

        def fetch(place):
            beside = jnp.where(here, first_ref[row, place], first_mate_ref[row, place])
            return jnp.where(gap == 0, own_ref[row, place], beside).astype(F32)

        sides = fetch(source)
        sides = jnp.concatenate([sides[:8], sides[8:]], axis=1)
        sides = jnp.where(slot < count_ref[leaf], sides, 0.0).astype(BF16)
        parts = fetch(4 + source)
        last = fetch(8)[:8]
        halves = []
        for half in range(2):
            part = parts[half * 8 : half * 8 + 8]
            tail = jnp.sum(
                jnp.where(row_ids == source * 2 + half, last, 0.0), axis=0, keepdims=True
            )
            place = (
                part[0:1] + part[3:4] + part[6:7],
                part[1:2] + part[4:5] + part[7:8],
                part[2:3] + part[5:6] + tail,
            )
            halves.append([jnp.broadcast_to(line, (8, 128)) for line in place])
        return sides, halves

    for leaf in range(4):
        own = points_ref[:, leaf * 256 : leaf * 256 + 256]
        own = jnp.concatenate([own, jnp.zeros((5, 256), F32)], axis=0).T
        for axis in range(3):
            wide = jnp.broadcast_to(own[:, axis : axis + 1], (256, 128))
            wide_ref[leaf, axis] = wide.reshape(32, 8, 128)

    def leaf_step(leaf, carry):
        total = jnp.zeros((8, 256), F32)
        for slot in range(8):
            sides, halves = source_of(leaf, slot)
            bands = []
            for band in range(0, 32, 8):
                tiles = []
                target = [wide_ref[leaf, axis, band : band + 8] for axis in range(3)]
                for place in halves:
                    first = target[0] - place[0]
                    second = target[1] - place[1]
                    third = target[2] - place[2]
                    dist_sq = first * first + second * second + third * third
                    inverse = lax.rsqrt(dist_sq * scale + floor)
                    tiles.append(inverse.reshape(64, 128).astype(BF16))
                bands.append(jnp.concatenate(tiles, axis=1))
            tile = jnp.concatenate(bands, axis=0)
            total += lax.dot_general(sides, tile, NT, preferred_element_type=F32)
        near_ref[leaf] = total
        return carry

    lax.fori_loop(0, 4, leaf_step, 0, unroll=4)


def couple(matrices, sources):
    slots = matrices.shape[0]
    products = lax.dot_general(
        matrices.reshape(slots * 64, 64), sources.astype(BF16), NT, preferred_element_type=F32
    )
    group = lax.broadcasted_iota(jnp.int32, (64, 128), 1) // 8
    total = jnp.zeros((64, 128), F32)
    for slot in range(slots):
        total = jnp.where(group == slot, products[slot * 64 : slot * 64 + 64], total)
    for shift in (64, 32, 16, 8):
        total = total + pltpu.roll(total, shift, 1)
    return total


def far_kernel(
    groups,
    cols,
    zs,
    coupling_list_ref,
    coupling_count_ref,
    coarse_list_ref,
    coarse_count_ref,
    owner_ref,
    own_ref,
    first_ref,
    first_mate_ref,
    last_ref,
    last_mate_ref,
    leaf_coupling_ref,
    coarse_coupling_ref,
    transfer_ref,
    basis_ref,
    near_ref,
    out_ref,
    source_ref,
):
    my_core = lax.axis_index("core")
    for slot in range(16):
        device = owner_ref[coarse_list_ref[0, slot]]
        row = lax.shift_right_logical(device, cols.bit_length() - 1)
        col = (device & (cols - 1)) ^ (zs // 2)
        tile_id = (row >> 1) * (cols // 4) + (col >> 2)
        mine = (row & 1) == my_core
        tile = jnp.where(mine, last_ref[tile_id], last_mate_ref[tile_id]).astype(F32)
        place = col & 3
        picked = tile[0:4]
        for step in range(1, 4):
            picked = jnp.where(place == step, tile[step * 4 : step * 4 + 4], picked)
        picked = jnp.where(slot < coarse_count_ref[0], picked, 0.0)
        source_ref[slot * 8 : slot * 8 + 8, :] = jnp.concatenate(
            [picked[:, :64], picked[:, 64:]], axis=0
        )
    coarse_field = couple(coarse_coupling_ref[0], source_ref[...])
    for leaf in range(4):
        for slot in range(16):
            row, gap, here, source = locate(coupling_list_ref[leaf, slot], cols)
            far = jnp.abs(gap)
            beyond = groups + row * 2 + jnp.where(far == 3, 1, 0)
            one = jnp.where(here, first_ref[row, 9], first_mate_ref[row, 9])
            more = jnp.where(here, last_ref[beyond], last_mate_ref[beyond])
            tile = jnp.where(far == 0, own_ref[row, 9], jnp.where(far == 1, one, more))
            tile = tile.astype(F32)
            half = jnp.where(source >= 2, tile[8:], tile[:8])
            half = jnp.where(source & 1 == 1, half[:, 64:], half[:, :64])
            live = slot < coupling_count_ref[leaf]
            source_ref[slot * 8 : slot * 8 + 8, :] = jnp.where(live, half, 0.0)
        local = couple(leaf_coupling_ref[leaf], source_ref[...])
        local = local + jnp.dot(
            transfer_ref[leaf].astype(F32),
            coarse_field,
            precision=lax.Precision.HIGHEST,
            preferred_element_type=F32,
        )
        local = local.T[:8].astype(BF16)
        far_part = lax.dot_general(local, basis_ref[leaf], NN, preferred_element_type=F32)
        span = slice(leaf * 256, leaf * 256 + 256)
        out_ref[:, span] = (near_ref[leaf] + far_part).astype(BF16)


VMEM = pl.BlockSpec(memory_space=pltpu.VMEM)
SMEM = pl.BlockSpec(memory_space=pltpu.SMEM)
PARAMS = pltpu.CompilerParams(vmem_limit_bytes=16 * 2**20)


def near_call(cols, *operands):
    return pl.pallas_call(
        functools.partial(near_kernel, cols),
        out_shape=jax.ShapeDtypeStruct((4, 8, 256), F32),
        in_specs=[SMEM] * 2 + [VMEM] * 4,
        out_specs=VMEM,
        scratch_shapes=[pltpu.VMEM((4, 3, 32, 8, 128), F32)],
        compiler_params=PARAMS,
        name="near",
        cost_estimate=pl.CostEstimate(
            flops=4_000_000_000, bytes_accessed=1_200_000, transcendentals=0
        ),
    )(*operands)


def far_call(groups, cols, zs, *operands):
    return pl.pallas_call(
        functools.partial(far_kernel, groups, cols, zs),
        out_shape=jax.ShapeDtypeStruct((8, 1024), BF16),
        in_specs=[SMEM] * 5 + [VMEM] * 10,
        out_specs=VMEM,
        scratch_shapes=[pltpu.VMEM((128, 64), F32)],
        compiler_params=PARAMS,
        name="far",
    )(*operands)


def per_device(
    xs,
    ys,
    zs,
    rhs,
    points,
    basis,
    transfer,
    leaf_coupling,
    coupling_list,
    coupling_count,
    coarse_coupling,
    coarse_list,
    coarse_count,
    owner,
    near_list,
    near_count,
):
    rows = 2 * xs
    cols = ys * zs
    row_axes = ("x", "core")
    swap = [(0, 1), (1, 0)]
    groups = xs * cols // 4
    turned = [(place + zs // 2) % zs for place in range(zs)]
    basis = jnp.swapaxes(basis, 1, 2)

    own, cluster = pl.pallas_call(
        pack_kernel,
        out_shape=(
            jax.ShapeDtypeStruct((rows, BLOCK, 16, 128), BF16),
            jax.ShapeDtypeStruct((zs, 4, 128), BF16),
        ),
        in_specs=[VMEM] * 4,
        out_specs=(VMEM, VMEM),
        compiler_params=PARAMS,
        name="pack",
    )(rhs, points, basis, transfer)

    def beside(step):
        pairs = []
        for core in range(2):
            for col in range(cols):
                source = col + step if core == 0 else col - step
                if 0 <= source < cols:
                    pairs.append((core * cols + source, core * cols + col))
        return pairs

    own = lax.all_to_all(own, row_axes, 0, 0, tiled=True)
    first = lax.ppermute(own, ("core", "y", "z"), beside(1))
    own, cluster = lax.optimization_barrier((own, cluster))
    line = lax.all_to_all(
        cluster, "z", 0, 0, tiled=True, axis_index_groups=[turned]
    ).reshape(zs // 4, 16, 128)
    first, line = lax.optimization_barrier((first, line))
    first_mate = lax.ppermute(first, "core", swap)
    coeffs = jnp.concatenate([own[:, 9:], first[:, 9:]], axis=1)
    second = lax.ppermute(coeffs, ("core", "y", "z"), beside(2))
    line = jnp.broadcast_to(line[None], (xs * ys,) + line.shape)
    same = lax.all_to_all(line, ("x", "y"), 0, 0, tiled=True).reshape(groups, 16, 128)

    near = near_call(cols, near_list, near_count, points, own, first, first_mate)
    same, second, near = lax.optimization_barrier((same, second, near))
    last = jnp.concatenate([same, second.reshape(rows * 2, 16, 128)], axis=0)
    last_mate = lax.ppermute(last, "core", swap)

    return far_call(
        groups,
        cols,
        zs,
        coupling_list,
        coupling_count,
        coarse_list,
        coarse_count,
        owner,
        own,
        first,
        first_mate,
        last,
        last_mate,
        leaf_coupling,
        coarse_coupling,
        transfer,
        basis,
        near,
    )


def solution(mesh):
    rows, cols = mesh.devices.shape
    xs, ys = rows // 2, 4
    zs = cols // ys
    axes = ("x", "core", "y", "z")
    fine = Mesh(mesh.devices.reshape(xs, 2, ys, zs), axes)
    in_specs = (
        P(None, axes),
        P(None, axes),
        P(axes, None, None),
        P(axes, None, None),
        P(axes, None, None, None),
        P(axes, None),
        P(axes),
        P(axes, None, None, None),
        P(axes, None),
        P(axes),
        P(),
        P(axes, None),
        P(axes),
    )
    return jax.shard_map(
        functools.partial(per_device, xs, ys, zs),
        mesh=fine,
        in_specs=in_specs,
        out_specs=P(None, axes),
        check_vma=False,
    )
```

```python
import functools

import jax
import jax.numpy as jnp
from jax import lax
from jax.experimental import pallas as pl
from jax.experimental.pallas import tpu as pltpu
from jax.sharding import Mesh, PartitionSpec as P

FOUR_PI = 12.566370614359172
SOFTEN = 0.0025
F32 = jnp.float32
BF16 = jnp.bfloat16
NN = (((1,), (0,)), ((), ()))
NT = (((1,), (1,)), ((), ()))

BLOCK = 10


def fetch_all(sources, targets, done_ref):
    copies = [
        pltpu.make_async_copy(source, target, done_ref.at[place])
        for place, (source, target) in enumerate(zip(sources, targets))
    ]
    for copy in copies:
        copy.start()
    for copy in copies:
        copy.wait()


def pack_kernel(
    rhs_hbm,
    points_hbm,
    basis_hbm,
    transfer_hbm,
    copies_ref,
    cluster_ref,
    rhs_ref,
    points_ref,
    basis_ref,
    transfer_ref,
    done_ref,
):
    fetch_all(
        (rhs_hbm, points_hbm, basis_hbm, transfer_hbm),
        (rhs_ref, points_ref, basis_ref, transfer_ref),
        done_ref,
    )
    block_ref = copies_ref.at[0]
    points = points_ref[...]
    part_hi = points.astype(BF16).astype(F32)
    rest = points - part_hi
    part_mid = rest.astype(BF16).astype(F32)
    part_lo = rest - part_mid
    parts = jnp.concatenate([part_hi, part_mid, part_lo[:2]], axis=0)
    cluster = jnp.zeros((8, 64), F32)
    coeffs = []
    last_rows = []
    for leaf in range(4):
        low = slice(leaf * 256, leaf * 256 + 128)
        high = slice(leaf * 256 + 128, leaf * 256 + 256)
        sides = rhs_ref[:, leaf * 256 : leaf * 256 + 256]
        coeff = lax.dot_general(sides, basis_ref[leaf], NT, preferred_element_type=F32)
        coeff = coeff.astype(BF16)
        cluster = cluster + jnp.dot(coeff, transfer_ref[leaf], preferred_element_type=F32)
        coeffs.append(coeff.astype(F32))
        wide = sides.astype(F32)
        block_ref[leaf] = jnp.concatenate([wide[:, :128], wide[:, 128:]], axis=0).astype(BF16)
        block_ref[4 + leaf] = jnp.concatenate([parts[:, low], parts[:, high]], axis=0).astype(BF16)
        last_rows += [part_lo[2:3, low], part_lo[2:3, high]]
    block_ref[8] = jnp.concatenate(last_rows + [jnp.zeros((8, 128), F32)], axis=0).astype(BF16)
    block_ref[9] = jnp.concatenate(
        [jnp.concatenate(coeffs[:2], axis=1), jnp.concatenate(coeffs[2:], axis=1)], axis=0
    ).astype(BF16)
    block = block_ref[...]
    for copy in range(1, copies_ref.shape[0]):
        copies_ref[copy] = block
    packed = jnp.concatenate([cluster[:4], cluster[4:]], axis=1).astype(BF16)
    cluster_ref[...] = jnp.broadcast_to(packed[None], cluster_ref.shape)


def locate(leaf_id, cols):
    device = lax.shift_right_logical(leaf_id, 2)
    row = lax.shift_right_logical(device, cols.bit_length() - 1)
    gap = (device & (cols - 1)) - lax.axis_index(("y", "z"))
    fetched_here = (gap > 0) == (lax.axis_index("core") == 0)
    return row, gap, fetched_here, leaf_id & 3


def near_kernel(
    cols,
    list_ref,
    count_ref,
    points_ref,
    own_ref,
    first_ref,
    first_mate_ref,
    near_ref,
    wide_ref,
):
    scale = F32(FOUR_PI * FOUR_PI)
    floor = F32(FOUR_PI * FOUR_PI * SOFTEN)
    row_ids = lax.broadcasted_iota(jnp.int32, (8, 128), 0)

    def source_of(leaf, slot):
        row, gap, here, source = locate(list_ref[leaf, slot], cols)

        def fetch(place):
            beside = jnp.where(here, first_ref[row, place], first_mate_ref[row, place])
            return jnp.where(gap == 0, own_ref[row, place], beside).astype(F32)

        sides = fetch(source)
        sides = jnp.concatenate([sides[:8], sides[8:]], axis=1)
        sides = jnp.where(slot < count_ref[leaf], sides, 0.0).astype(BF16)
        parts = fetch(4 + source)
        last = fetch(8)[:8]
        halves = []
        for half in range(2):
            part = parts[half * 8 : half * 8 + 8]
            tail = jnp.sum(
                jnp.where(row_ids == source * 2 + half, last, 0.0), axis=0, keepdims=True
            )
            place = (
                part[0:1] + part[3:4] + part[6:7],
                part[1:2] + part[4:5] + part[7:8],
                part[2:3] + part[5:6] + tail,
            )
            halves.append([jnp.broadcast_to(line, (8, 128)) for line in place])
        return sides, halves

    for leaf in range(4):
        own = points_ref[:, leaf * 256 : leaf * 256 + 256]
        own = jnp.concatenate([own, jnp.zeros((5, 256), F32)], axis=0).T
        for axis in range(3):
            wide = jnp.broadcast_to(own[:, axis : axis + 1], (256, 128))
            wide_ref[leaf, axis] = wide.reshape(32, 8, 128)

    def leaf_step(leaf, carry):
        total = jnp.zeros((8, 256), F32)
        for slot in range(8):
            sides, halves = source_of(leaf, slot)
            bands = []
            for band in range(0, 32, 8):
                tiles = []
                target = [wide_ref[leaf, axis, band : band + 8] for axis in range(3)]
                for place in halves:
                    first = target[0] - place[0]
                    second = target[1] - place[1]
                    third = target[2] - place[2]
                    dist_sq = first * first + second * second + third * third
                    inverse = lax.rsqrt(dist_sq * scale + floor)
                    tiles.append(inverse.reshape(64, 128).astype(BF16))
                bands.append(jnp.concatenate(tiles, axis=1))
            tile = jnp.concatenate(bands, axis=0)
            total += lax.dot_general(sides, tile, NT, preferred_element_type=F32)
        near_ref[leaf] = total
        return carry

    lax.fori_loop(0, 4, leaf_step, 0, unroll=4)


def couple(matrices, sources):
    slots = matrices.shape[0]
    products = lax.dot_general(
        matrices.reshape(slots * 64, 64), sources.astype(BF16), NT, preferred_element_type=F32
    )
    group = lax.broadcasted_iota(jnp.int32, (64, 128), 1) // 8
    total = products[:64]
    for slot in range(1, slots):
        total = jnp.where(group == slot, products[slot * 64 : slot * 64 + 64], total)
    return total


def sum_groups(total):
    for shift in (64, 32, 16, 8):
        total = total + pltpu.roll(total, shift, 1)
    return total


def far_kernel(
    groups,
    cols,
    zs,
    coupling_list_ref,
    coupling_count_ref,
    coarse_list_ref,
    coarse_count_ref,
    owner_ref,
    own_ref,
    first_ref,
    first_mate_ref,
    last_ref,
    last_mate_ref,
    leaf_coupling_ref,
    coarse_coupling_ref,
    transfer_ref,
    basis_ref,
    near_ref,
    out_ref,
    source_ref,
):
    my_core = lax.axis_index("core")
    for slot in range(16):
        device = owner_ref[coarse_list_ref[0, slot]]
        row = lax.shift_right_logical(device, cols.bit_length() - 1)
        col = device & (cols - 1)
        z = col & (zs - 1)
        order = jnp.where(z < zs // 2, z * 2, (zs - z) * 2 + 1)
        order = jnp.where(z == 0, 1, jnp.where(z == zs // 2, 0, order))
        tile_id = (row >> 1) * (cols // 4) + ((col - z + order) >> 2)
        mine = (row & 1) == my_core
        tile = jnp.where(mine, last_ref[tile_id], last_mate_ref[tile_id]).astype(F32)
        place = order & 3
        picked = tile[0:4]
        for step in range(1, 4):
            picked = jnp.where(place == step, tile[step * 4 : step * 4 + 4], picked)
        picked = jnp.where(slot < coarse_count_ref[0], picked, 0.0)
        source_ref[4, slot * 8 : slot * 8 + 8, :] = jnp.concatenate(
            [picked[:, :64], picked[:, 64:]], axis=0
        )
    for leaf in range(4):
        for slot in range(16):
            row, gap, here, source = locate(coupling_list_ref[leaf, slot], cols)
            far = jnp.abs(gap)
            beyond = groups + row * 2 + jnp.where(far == 3, 1, 0)
            one = jnp.where(here, first_ref[row, 9], first_mate_ref[row, 9])
            more = jnp.where(here, last_ref[beyond], last_mate_ref[beyond])
            tile = jnp.where(far == 0, own_ref[row, 9], jnp.where(far == 1, one, more))
            tile = tile.astype(F32)
            half = jnp.where(source >= 2, tile[8:], tile[:8])
            half = jnp.where(source & 1 == 1, half[:, 64:], half[:, :64])
            live = slot < coupling_count_ref[leaf]
            source_ref[leaf, slot * 8 : slot * 8 + 8, :] = jnp.where(live, half, 0.0)
    totals = [couple(leaf_coupling_ref[leaf], source_ref[leaf]) for leaf in range(4)]
    coarse_field = sum_groups(couple(coarse_coupling_ref[0], source_ref[4]))
    field_hi = coarse_field.astype(BF16).astype(F32)
    rest = coarse_field - field_hi
    field_mid = rest.astype(BF16).astype(F32)
    group = lax.broadcasted_iota(jnp.int32, (64, 128), 1) // 8
    parts = jnp.where(group == 2, rest - field_mid, 0.0)
    parts = jnp.where(group == 1, field_mid, jnp.where(group == 0, field_hi, parts)).astype(BF16)
    for leaf in range(4):
        totals[leaf] += jnp.dot(transfer_ref[leaf], parts, preferred_element_type=F32)
    local = sum_groups(jnp.concatenate(totals, axis=0)).T[:8]
    for leaf in range(4):
        mine = local[:, leaf * 64 : leaf * 64 + 64].astype(BF16)
        far_part = lax.dot_general(mine, basis_ref[leaf], NN, preferred_element_type=F32)
        span = slice(leaf * 256, leaf * 256 + 256)
        out_ref[:, span] = (near_ref[leaf] + far_part).astype(BF16)


VMEM = pl.BlockSpec(memory_space=pltpu.VMEM)
ANY = pl.BlockSpec(memory_space=pl.ANY)
SMEM = pl.BlockSpec(memory_space=pltpu.SMEM)
PARAMS = pltpu.CompilerParams(vmem_limit_bytes=16 * 2**20)


def near_call(cols, *operands):
    return pl.pallas_call(
        functools.partial(near_kernel, cols),
        out_shape=jax.ShapeDtypeStruct((4, 8, 256), F32),
        in_specs=[SMEM] * 2 + [VMEM] * 4,
        out_specs=VMEM,
        scratch_shapes=[pltpu.VMEM((4, 3, 32, 8, 128), F32)],
        compiler_params=PARAMS,
        name="near",
        cost_estimate=pl.CostEstimate(
            flops=4_000_000_000, bytes_accessed=1_200_000, transcendentals=0
        ),
    )(*operands)


def far_call(groups, cols, zs, *operands):
    return pl.pallas_call(
        functools.partial(far_kernel, groups, cols, zs),
        out_shape=jax.ShapeDtypeStruct((8, 1024), BF16),
        in_specs=[SMEM] * 5 + [VMEM] * 10,
        out_specs=VMEM,
        scratch_shapes=[pltpu.VMEM((5, 128, 64), F32)],
        compiler_params=PARAMS,
        name="far",
    )(*operands)


def per_device(
    xs,
    ys,
    zs,
    rhs,
    points,
    basis,
    transfer,
    leaf_coupling,
    coupling_list,
    coupling_count,
    coarse_coupling,
    coarse_list,
    coarse_count,
    owner,
    near_list,
    near_count,
):
    rows = 2 * xs
    cols = ys * zs
    row_axes = ("x", "core")
    swap = [(0, 1), (1, 0)]
    groups = xs * cols // 4
    half = zs // 2
    turned = [half, 0] + [z for near in range(1, half) for z in (near, zs - near)]
    basis = jnp.swapaxes(basis, 1, 2)

    own, cluster = pl.pallas_call(
        pack_kernel,
        out_shape=(
            jax.ShapeDtypeStruct((rows, BLOCK, 16, 128), BF16),
            jax.ShapeDtypeStruct((zs, 4, 128), BF16),
        ),
        in_specs=[ANY] * 4,
        out_specs=(VMEM, VMEM),
        scratch_shapes=[
            pltpu.VMEM(rhs.shape, BF16),
            pltpu.VMEM(points.shape, F32),
            pltpu.VMEM(basis.shape, BF16),
            pltpu.VMEM(transfer.shape, BF16),
            pltpu.SemaphoreType.DMA((4,)),
        ],
        name="pack",
    )(rhs, points, basis, transfer)

    def beside(step):
        pairs = []
        for core in range(2):
            for col in range(cols):
                source = col + step if core == 0 else col - step
                if 0 <= source < cols:
                    pairs.append((core * cols + source, core * cols + col))
        return pairs

    own = lax.all_to_all(own, row_axes, 0, 0, tiled=True)
    first = lax.ppermute(own, ("core", "y", "z"), beside(1))
    own, cluster = lax.optimization_barrier((own, cluster))
    line = lax.all_to_all(
        cluster, "z", 0, 0, tiled=True, axis_index_groups=[turned]
    ).reshape(zs // 4, 16, 128)
    first, line = lax.optimization_barrier((first, line))
    first_mate = lax.ppermute(first, "core", swap)
    coeffs = jnp.concatenate([own[:, 9:], first[:, 9:]], axis=1)
    second = lax.ppermute(coeffs, ("core", "y", "z"), beside(2))
    line = jnp.broadcast_to(line[None], (xs * ys,) + line.shape)
    same = lax.all_to_all(line, ("x", "y"), 0, 0, tiled=True).reshape(groups, 16, 128)

    near = near_call(cols, near_list, near_count, points, own, first, first_mate)
    same, second, near = lax.optimization_barrier((same, second, near))
    last = jnp.concatenate([same, second.reshape(rows * 2, 16, 128)], axis=0)
    last_mate = lax.ppermute(last, "core", swap)

    return far_call(
        groups,
        cols,
        zs,
        coupling_list,
        coupling_count,
        coarse_list,
        coarse_count,
        owner,
        own,
        first,
        first_mate,
        last,
        last_mate,
        leaf_coupling,
        coarse_coupling,
        transfer,
        basis,
        near,
    )


def solution(mesh):
    rows, cols = mesh.devices.shape
    xs, ys = rows // 2, 4
    zs = cols // ys
    axes = ("x", "core", "y", "z")
    fine = Mesh(mesh.devices.reshape(xs, 2, ys, zs), axes)
    in_specs = (
        P(None, axes),
        P(None, axes),
        P(axes, None, None),
        P(axes, None, None),
        P(axes, None, None, None),
        P(axes, None),
        P(axes),
        P(axes, None, None, None),
        P(axes, None),
        P(axes),
        P(),
        P(axes, None),
        P(axes),
    )
    return jax.shard_map(
        functools.partial(per_device, xs, ys, zs),
        mesh=fine,
        in_specs=in_specs,
        out_specs=P(None, axes),
        check_vma=False,
    )
```

```python
import functools

import jax
import jax.numpy as jnp
from jax import lax
from jax.experimental import pallas as pl
from jax.experimental.pallas import tpu as pltpu
from jax.sharding import Mesh, PartitionSpec as P

FOUR_PI = 12.566370614359172
SOFTEN = 0.0025
F32 = jnp.float32
BF16 = jnp.bfloat16
NN = (((1,), (0,)), ((), ()))
NT = (((1,), (1,)), ((), ()))

BLOCK = 10


def fetch_all(sources, targets, done_ref):
    copies = [
        pltpu.make_async_copy(source, target, done_ref.at[place])
        for place, (source, target) in enumerate(zip(sources, targets))
    ]
    for copy in copies:
        copy.start()
    for copy in copies:
        copy.wait()


def pack_kernel(
    rhs_hbm,
    points_hbm,
    basis_hbm,
    transfer_hbm,
    copies_ref,
    cluster_ref,
    rhs_ref,
    points_ref,
    basis_ref,
    transfer_ref,
    done_ref,
):
    fetch_all(
        (rhs_hbm, points_hbm, basis_hbm, transfer_hbm),
        (rhs_ref, points_ref, basis_ref, transfer_ref),
        done_ref,
    )
    block_ref = copies_ref.at[0]
    points = points_ref[...]
    part_hi = points.astype(BF16).astype(F32)
    rest = points - part_hi
    part_mid = rest.astype(BF16).astype(F32)
    part_lo = rest - part_mid
    parts = jnp.concatenate([part_hi, part_mid, part_lo[:2]], axis=0)
    cluster = jnp.zeros((8, 64), F32)
    coeffs = []
    last_rows = []
    for leaf in range(4):
        low = slice(leaf * 256, leaf * 256 + 128)
        high = slice(leaf * 256 + 128, leaf * 256 + 256)
        sides = rhs_ref[:, leaf * 256 : leaf * 256 + 256]
        coeff = lax.dot_general(sides, basis_ref[leaf], NT, preferred_element_type=F32)
        coeff = coeff.astype(BF16)
        cluster = cluster + jnp.dot(coeff, transfer_ref[leaf], preferred_element_type=F32)
        coeffs.append(coeff.astype(F32))
        wide = sides.astype(F32)
        block_ref[leaf] = jnp.concatenate([wide[:, :128], wide[:, 128:]], axis=0).astype(BF16)
        block_ref[4 + leaf] = jnp.concatenate([parts[:, low], parts[:, high]], axis=0).astype(BF16)
        last_rows += [part_lo[2:3, low], part_lo[2:3, high]]
    block_ref[8] = jnp.concatenate(last_rows + [jnp.zeros((8, 128), F32)], axis=0).astype(BF16)
    block_ref[9] = jnp.concatenate(
        [jnp.concatenate(coeffs[:2], axis=1), jnp.concatenate(coeffs[2:], axis=1)], axis=0
    ).astype(BF16)
    copies_ref[1] = block_ref[...]
    packed = jnp.concatenate([cluster[:4], cluster[4:]], axis=1).astype(BF16)
    cluster_ref[...] = jnp.broadcast_to(packed[None], cluster_ref.shape)


def locate(leaf_id, cols):
    device = lax.shift_right_logical(leaf_id, 2)
    row = lax.shift_right_logical(device, cols.bit_length() - 1)
    chip_gap = (row >> 1) - lax.axis_index("x")
    gap = (device & (cols - 1)) - lax.axis_index(("y", "z"))
    return chip_gap, row & 1, gap, leaf_id & 3


def near_kernel(
    cols,
    list_ref,
    count_ref,
    points_ref,
    window_ref,
    beside_ref,
    near_ref,
    wide_ref,
):
    scale = F32(FOUR_PI * FOUR_PI)
    floor = F32(FOUR_PI * FOUR_PI * SOFTEN)
    row_ids = lax.broadcasted_iota(jnp.int32, (8, 128), 0)

    def source_of(leaf, slot):
        chip_gap, row, gap, source = locate(list_ref[leaf, slot], cols)
        holder = jnp.where(gap == 0, row, jnp.where(gap > 0, 0, 1))
        base = jnp.where(gap == 0, 0, BLOCK + row * BLOCK)

        def fetch(place):
            here = window_ref[holder, base + place]
            return jnp.where(chip_gap == 0, here, beside_ref[holder, base + place]).astype(F32)

        sides = fetch(source)
        sides = jnp.concatenate([sides[:8], sides[8:]], axis=1)
        sides = jnp.where(slot < count_ref[leaf], sides, 0.0).astype(BF16)
        parts = fetch(4 + source)
        last = fetch(8)[:8]
        halves = []
        for half in range(2):
            part = parts[half * 8 : half * 8 + 8]
            tail = jnp.sum(
                jnp.where(row_ids == source * 2 + half, last, 0.0), axis=0, keepdims=True
            )
            place = (
                part[0:1] + part[3:4] + part[6:7],
                part[1:2] + part[4:5] + part[7:8],
                part[2:3] + part[5:6] + tail,
            )
            halves.append([jnp.broadcast_to(line, (8, 128)) for line in place])
        return sides, halves

    for leaf in range(4):
        own = points_ref[:, leaf * 256 : leaf * 256 + 256]
        own = jnp.concatenate([own, jnp.zeros((5, 256), F32)], axis=0).T
        for axis in range(3):
            wide = jnp.broadcast_to(own[:, axis : axis + 1], (256, 128))
            wide_ref[leaf, axis] = wide.reshape(32, 8, 128)

    def leaf_step(leaf, carry):
        total = jnp.zeros((8, 256), F32)
        for slot in range(8):
            sides, halves = source_of(leaf, slot)
            bands = []
            for band in range(0, 32, 8):
                tiles = []
                target = [wide_ref[leaf, axis, band : band + 8] for axis in range(3)]
                for place in halves:
                    first = target[0] - place[0]
                    second = target[1] - place[1]
                    third = target[2] - place[2]
                    dist_sq = first * first + second * second + third * third
                    inverse = lax.rsqrt(dist_sq * scale + floor)
                    tiles.append(inverse.reshape(64, 128).astype(BF16))
                bands.append(jnp.concatenate(tiles, axis=1))
            tile = jnp.concatenate(bands, axis=0)
            total += lax.dot_general(sides, tile, NT, preferred_element_type=F32)
        near_ref[leaf] = total
        return carry

    lax.fori_loop(0, 4, leaf_step, 0, unroll=4)


def couple(matrices, sources):
    slots = matrices.shape[0]
    products = lax.dot_general(
        matrices.reshape(slots * 64, 64), sources.astype(BF16), NT, preferred_element_type=F32
    )
    group = lax.broadcasted_iota(jnp.int32, (64, 128), 1) // 8
    total = products[:64]
    for slot in range(1, slots):
        total = jnp.where(group == slot, products[slot * 64 : slot * 64 + 64], total)
    return total


def sum_groups(total):
    for shift in (64, 32, 16, 8):
        total = total + pltpu.roll(total, shift, 1)
    return total


def far_kernel(
    groups,
    cols,
    zs,
    coupling_list_ref,
    coupling_count_ref,
    coarse_list_ref,
    coarse_count_ref,
    owner_ref,
    coeffs_ref,
    last_ref,
    last_mate_ref,
    beyond_ref,
    leaf_coupling_ref,
    coarse_coupling_ref,
    transfer_ref,
    basis_ref,
    near_ref,
    out_ref,
    source_ref,
):
    my_core = lax.axis_index("core")
    for slot in range(16):
        device = owner_ref[coarse_list_ref[0, slot]]
        row = lax.shift_right_logical(device, cols.bit_length() - 1)
        col = device & (cols - 1)
        z = col & (zs - 1)
        order = jnp.where(z < zs // 2, z * 2, (zs - z) * 2 + 1)
        order = jnp.where(z == 0, 1, jnp.where(z == zs // 2, 0, order))
        tile_id = (row >> 1) * (cols // 4) + ((col - z + order) >> 2)
        mine = (row & 1) == my_core
        tile = jnp.where(mine, last_ref[tile_id], last_mate_ref[tile_id]).astype(F32)
        place = order & 3
        picked = tile[0:4]
        for step in range(1, 4):
            picked = jnp.where(place == step, tile[step * 4 : step * 4 + 4], picked)
        picked = jnp.where(slot < coarse_count_ref[0], picked, 0.0)
        source_ref[4, slot * 8 : slot * 8 + 8, :] = jnp.concatenate(
            [picked[:, :64], picked[:, 64:]], axis=0
        )
    for leaf in range(4):
        for slot in range(16):
            chip_gap, row, gap, source = locate(coupling_list_ref[leaf, slot], cols)
            far = jnp.abs(gap)
            place = jnp.where(far == 1, 1 + row, 1 + row * 2 + far) + jnp.where(gap < 0, 7, 0)
            place = jnp.where(far == 0, row * 7, place)
            fetched_here = (chip_gap < 0) == (my_core == 0)
            tile = jnp.where(fetched_here, last_ref[groups + place], last_mate_ref[groups + place])
            tile = jnp.where(jnp.abs(chip_gap) == 2, beyond_ref[place], tile)
            tile = jnp.where(chip_gap == 0, coeffs_ref[place], tile).astype(F32)
            half = jnp.where(source >= 2, tile[8:], tile[:8])
            half = jnp.where(source & 1 == 1, half[:, 64:], half[:, :64])
            live = slot < coupling_count_ref[leaf]
            source_ref[leaf, slot * 8 : slot * 8 + 8, :] = jnp.where(live, half, 0.0)
    totals = [couple(leaf_coupling_ref[leaf], source_ref[leaf]) for leaf in range(4)]
    coarse_field = sum_groups(couple(coarse_coupling_ref[0], source_ref[4]))
    field_hi = coarse_field.astype(BF16).astype(F32)
    rest = coarse_field - field_hi
    field_mid = rest.astype(BF16).astype(F32)
    group = lax.broadcasted_iota(jnp.int32, (64, 128), 1) // 8
    parts = jnp.where(group == 2, rest - field_mid, 0.0)
    parts = jnp.where(group == 1, field_mid, jnp.where(group == 0, field_hi, parts)).astype(BF16)
    for leaf in range(4):
        totals[leaf] += jnp.dot(transfer_ref[leaf], parts, preferred_element_type=F32)
    local = sum_groups(jnp.concatenate(totals, axis=0)).T[:8]
    for leaf in range(4):
        mine = local[:, leaf * 64 : leaf * 64 + 64].astype(BF16)
        far_part = lax.dot_general(mine, basis_ref[leaf], NN, preferred_element_type=F32)
        span = slice(leaf * 256, leaf * 256 + 256)
        out_ref[:, span] = (near_ref[leaf] + far_part).astype(BF16)


VMEM = pl.BlockSpec(memory_space=pltpu.VMEM)
ANY = pl.BlockSpec(memory_space=pl.ANY)
SMEM = pl.BlockSpec(memory_space=pltpu.SMEM)
PARAMS = pltpu.CompilerParams(vmem_limit_bytes=16 * 2**20)


def near_call(cols, *operands):
    return pl.pallas_call(
        functools.partial(near_kernel, cols),
        out_shape=jax.ShapeDtypeStruct((4, 8, 256), F32),
        in_specs=[SMEM] * 2 + [VMEM] * 3,
        out_specs=VMEM,
        scratch_shapes=[pltpu.VMEM((4, 3, 32, 8, 128), F32)],
        compiler_params=PARAMS,
        name="near",
        cost_estimate=pl.CostEstimate(
            flops=4_000_000_000, bytes_accessed=1_200_000, transcendentals=0
        ),
    )(*operands)


def far_call(groups, cols, zs, *operands):
    return pl.pallas_call(
        functools.partial(far_kernel, groups, cols, zs),
        out_shape=jax.ShapeDtypeStruct((8, 1024), BF16),
        in_specs=[SMEM] * 5 + [VMEM] * 9,
        out_specs=VMEM,
        scratch_shapes=[pltpu.VMEM((5, 128, 64), F32)],
        compiler_params=PARAMS,
        name="far",
    )(*operands)


def per_device(
    xs,
    ys,
    zs,
    rhs,
    points,
    basis,
    transfer,
    leaf_coupling,
    coupling_list,
    coupling_count,
    coarse_coupling,
    coarse_list,
    coarse_count,
    owner,
    near_list,
    near_count,
):
    cols = ys * zs
    groups = xs * cols // 4
    half = zs // 2
    turned = [half, 0] + [z for near in range(1, half) for z in (near, zs - near)]
    basis = jnp.swapaxes(basis, 1, 2)

    blocks, cluster = pl.pallas_call(
        pack_kernel,
        out_shape=(
            jax.ShapeDtypeStruct((2, BLOCK, 16, 128), BF16),
            jax.ShapeDtypeStruct((zs, 4, 128), BF16),
        ),
        in_specs=[ANY] * 4,
        out_specs=(VMEM, VMEM),
        scratch_shapes=[
            pltpu.VMEM(rhs.shape, BF16),
            pltpu.VMEM(points.shape, F32),
            pltpu.VMEM(basis.shape, BF16),
            pltpu.VMEM(transfer.shape, BF16),
            pltpu.SemaphoreType.DMA((4,)),
        ],
        name="pack",
    )(rhs, points, basis, transfer)

    def along_col(step):
        pairs = []
        for core in range(2):
            for col in range(cols):
                source = col + step if core == 0 else col - step
                if 0 <= source < cols:
                    pairs.append((core * cols + source, core * cols + col))
        return pairs

    def along_x(step):
        pairs = []
        for x in range(xs):
            for core in range(2):
                source = x - step if core == 0 else x + step
                if 0 <= source < xs:
                    pairs.append((source * 2 + core, x * 2 + core))
        return pairs

    def coeffs_of(window):
        parts = [window[:, place : place + 1] for place in (9, 19, 29)]
        return jnp.concatenate(parts + [window[:, 30:]], axis=1).reshape(14, 16, 128)

    chip = lax.all_gather(blocks, "core", axis=0, tiled=False)
    first = lax.ppermute(chip, ("core", "y", "z"), along_col(1))[:, 0]
    chip, cluster = lax.optimization_barrier((chip, cluster))
    line = lax.all_to_all(
        cluster, "z", 0, 0, tiled=True, axis_index_groups=[turned]
    ).reshape(zs // 4, 16, 128)
    first, line = lax.optimization_barrier((first, line))
    second = jnp.concatenate([chip[:, 0, 9:], first[:, 9:]], axis=1)
    second = lax.ppermute(second, ("core", "y", "z"), along_col(2))
    line = jnp.broadcast_to(line[None], (xs * ys,) + line.shape)
    same = lax.all_to_all(line, ("x", "y"), 0, 0, tiled=True).reshape(groups, 16, 128)

    window = jnp.concatenate(
        [blocks[0], first.reshape(2 * BLOCK, 16, 128), second.reshape(4, 16, 128)], axis=0
    )
    window = lax.all_gather(window, "core", axis=0, tiled=False)
    beside = lax.ppermute(window, ("x", "core"), along_x(1))
    coeffs = coeffs_of(window)
    beyond = lax.ppermute(coeffs, ("x", "core"), along_x(2))
    near = near_call(cols, near_list, near_count, points, window, beside)

    same, beside, beyond, near = lax.optimization_barrier((same, beside, beyond, near))
    last = jnp.concatenate([same, coeffs_of(beside)], axis=0)
    last_mate = lax.ppermute(last, "core", [(0, 1), (1, 0)])

    return far_call(
        groups,
        cols,
        zs,
        coupling_list,
        coupling_count,
        coarse_list,
        coarse_count,
        owner,
        coeffs,
        last,
        last_mate,
        beyond,
        leaf_coupling,
        coarse_coupling,
        transfer,
        basis,
        near,
    )


def solution(mesh):
    rows, cols = mesh.devices.shape
    xs, ys = rows // 2, 4
    zs = cols // ys
    axes = ("x", "core", "y", "z")
    fine = Mesh(mesh.devices.reshape(xs, 2, ys, zs), axes)
    in_specs = (
        P(None, axes),
        P(None, axes),
        P(axes, None, None),
        P(axes, None, None),
        P(axes, None, None, None),
        P(axes, None),
        P(axes),
        P(axes, None, None, None),
        P(axes, None),
        P(axes),
        P(),
        P(axes, None),
        P(axes),
    )
    return jax.shard_map(
        functools.partial(per_device, xs, ys, zs),
        mesh=fine,
        in_specs=in_specs,
        out_specs=P(None, axes),
        check_vma=False,
    )
```

```python
import functools

import jax
import jax.numpy as jnp
from jax import lax
from jax.experimental import pallas as pl
from jax.experimental.pallas import tpu as pltpu
from jax.sharding import Mesh, PartitionSpec as P

FOUR_PI = 12.566370614359172
SOFTEN = 0.0025
F32 = jnp.float32
BF16 = jnp.bfloat16
NN = (((1,), (0,)), ((), ()))
NT = (((1,), (1,)), ((), ()))

BLOCK = 10


def fetch_all(sources, targets, done_ref):
    copies = [
        pltpu.make_async_copy(source, target, done_ref.at[place])
        for place, (source, target) in enumerate(zip(sources, targets))
    ]
    for copy in copies:
        copy.start()
    for copy in copies:
        copy.wait()


def pack_kernel(
    rhs_hbm,
    points_hbm,
    basis_hbm,
    transfer_hbm,
    copies_ref,
    cluster_ref,
    rhs_ref,
    points_ref,
    basis_ref,
    transfer_ref,
    done_ref,
):
    fetch_all(
        (rhs_hbm, points_hbm, basis_hbm, transfer_hbm),
        (rhs_ref, points_ref, basis_ref, transfer_ref),
        done_ref,
    )
    block_ref = copies_ref.at[0]
    points = points_ref[...]
    part_hi = points.astype(BF16).astype(F32)
    rest = points - part_hi
    part_mid = rest.astype(BF16).astype(F32)
    part_lo = rest - part_mid
    parts = jnp.concatenate([part_hi, part_mid, part_lo[:2]], axis=0)
    cluster = jnp.zeros((8, 64), F32)
    coeffs = []
    last_rows = []
    for leaf in range(4):
        low = slice(leaf * 256, leaf * 256 + 128)
        high = slice(leaf * 256 + 128, leaf * 256 + 256)
        sides = rhs_ref[:, leaf * 256 : leaf * 256 + 256]
        coeff = lax.dot_general(sides, basis_ref[leaf], NT, preferred_element_type=F32)
        coeff = coeff.astype(BF16)
        cluster = cluster + jnp.dot(coeff, transfer_ref[leaf], preferred_element_type=F32)
        coeffs.append(coeff.astype(F32))
        wide = sides.astype(F32)
        block_ref[leaf] = jnp.concatenate([wide[:, :128], wide[:, 128:]], axis=0).astype(BF16)
        block_ref[4 + leaf] = jnp.concatenate([parts[:, low], parts[:, high]], axis=0).astype(BF16)
        last_rows += [part_lo[2:3, low], part_lo[2:3, high]]
    block_ref[8] = jnp.concatenate(last_rows + [jnp.zeros((8, 128), F32)], axis=0).astype(BF16)
    block_ref[9] = jnp.concatenate(
        [jnp.concatenate(coeffs[:2], axis=1), jnp.concatenate(coeffs[2:], axis=1)], axis=0
    ).astype(BF16)
    copies_ref[1] = block_ref[...]
    packed = jnp.concatenate([cluster[:4], cluster[4:]], axis=1).astype(BF16)
    cluster_ref[...] = jnp.broadcast_to(packed[None], cluster_ref.shape)


def locate(leaf_id, cols):
    device = lax.shift_right_logical(leaf_id, 2)
    row = lax.shift_right_logical(device, cols.bit_length() - 1)
    chip_gap = (row >> 1) - lax.axis_index("x")
    gap = (device & (cols - 1)) - lax.axis_index(("y", "z"))
    return chip_gap, row & 1, gap, leaf_id & 3


def near_kernel(
    cols,
    list_ref,
    count_ref,
    points_ref,
    window_ref,
    beside_ref,
    near_ref,
    wide_ref,
):
    scale = F32(FOUR_PI * FOUR_PI)
    floor = F32(FOUR_PI * FOUR_PI * SOFTEN)
    row_ids = lax.broadcasted_iota(jnp.int32, (8, 128), 0)

    def source_of(leaf, slot):
        chip_gap, row, gap, source = locate(list_ref[leaf, slot], cols)
        holder = jnp.where(gap == 0, row, jnp.where(gap > 0, 0, 1))
        base = jnp.where(gap == 0, 0, BLOCK + row * BLOCK)

        def fetch(place):
            here = window_ref[holder, base + place]
            return jnp.where(chip_gap == 0, here, beside_ref[holder, base + place]).astype(F32)

        sides = fetch(source)
        sides = jnp.concatenate([sides[:8], sides[8:]], axis=1)
        sides = jnp.where(slot < count_ref[leaf], sides, 0.0).astype(BF16)
        parts = fetch(4 + source)
        last = fetch(8)[:8]
        halves = []
        for half in range(2):
            part = parts[half * 8 : half * 8 + 8]
            tail = jnp.sum(
                jnp.where(row_ids == source * 2 + half, last, 0.0), axis=0, keepdims=True
            )
            place = (
                part[0:1] + part[3:4] + part[6:7],
                part[1:2] + part[4:5] + part[7:8],
                part[2:3] + part[5:6] + tail,
            )
            halves.append([jnp.broadcast_to(line, (8, 128)) for line in place])
        return sides, halves

    for leaf in range(4):
        own = points_ref[:, leaf * 256 : leaf * 256 + 256]
        own = jnp.concatenate([own, jnp.zeros((5, 256), F32)], axis=0).T
        for axis in range(3):
            wide = jnp.broadcast_to(own[:, axis : axis + 1], (256, 128))
            wide_ref[leaf, axis] = wide.reshape(32, 8, 128)

    def leaf_step(leaf, carry):
        total = jnp.zeros((8, 256), F32)
        for slot in range(8):
            sides, halves = source_of(leaf, slot)
            bands = []
            for band in range(0, 32, 8):
                tiles = []
                target = [wide_ref[leaf, axis, band : band + 8] for axis in range(3)]
                for place in halves:
                    first = target[0] - place[0]
                    second = target[1] - place[1]
                    third = target[2] - place[2]
                    dist_sq = first * first + second * second + third * third
                    inverse = lax.rsqrt(dist_sq * scale + floor)
                    tiles.append(inverse.reshape(64, 128).astype(BF16))
                bands.append(jnp.concatenate(tiles, axis=1))
            tile = jnp.concatenate(bands, axis=0)
            total += lax.dot_general(sides, tile, NT, preferred_element_type=F32)
        near_ref[leaf] = total
        return carry

    lax.fori_loop(0, 4, leaf_step, 0, unroll=4)


def couple(matrices, sources):
    slots = matrices.shape[0]
    products = lax.dot_general(
        matrices.reshape(slots * 64, 64), sources.astype(BF16), NT, preferred_element_type=F32
    )
    group = lax.broadcasted_iota(jnp.int32, (64, 128), 1) // 8
    total = products[:64]
    for slot in range(1, slots):
        total = jnp.where(group == slot, products[slot * 64 : slot * 64 + 64], total)
    return total


def sum_groups(total):
    for shift in (64, 32, 16, 8):
        total = total + pltpu.roll(total, shift, 1)
    return total


def far_kernel(
    groups,
    cols,
    zs,
    coupling_list_ref,
    coupling_count_ref,
    coarse_list_ref,
    coarse_count_ref,
    owner_ref,
    coeffs_ref,
    last_ref,
    last_mate_ref,
    beyond_ref,
    leaf_coupling_ref,
    coarse_coupling_ref,
    transfer_ref,
    basis_ref,
    near_ref,
    out_ref,
    source_ref,
):
    my_core = lax.axis_index("core")
    for slot in range(16):
        device = owner_ref[coarse_list_ref[0, slot]]
        row = lax.shift_right_logical(device, cols.bit_length() - 1)
        col = device & (cols - 1)
        z = col & (zs - 1)
        order = jnp.where(z < zs // 2, z * 2, (zs - z) * 2 + 1)
        order = jnp.where(z == 0, 1, jnp.where(z == zs // 2, 0, order))
        tile_id = (row >> 1) * (cols // 4) + ((col - z + order) >> 2)
        mine = (row & 1) == my_core
        tile = jnp.where(mine, last_ref[tile_id], last_mate_ref[tile_id]).astype(F32)
        place = order & 3
        picked = tile[0:4]
        for step in range(1, 4):
            picked = jnp.where(place == step, tile[step * 4 : step * 4 + 4], picked)
        picked = jnp.where(slot < coarse_count_ref[0], picked, 0.0)
        source_ref[4, slot * 8 : slot * 8 + 8, :] = jnp.concatenate(
            [picked[:, :64], picked[:, 64:]], axis=0
        )
    for leaf in range(4):
        for slot in range(16):
            chip_gap, row, gap, source = locate(coupling_list_ref[leaf, slot], cols)
            far = jnp.abs(gap)
            place = jnp.where(far == 1, 1 + row, 1 + row * 2 + far) + jnp.where(gap < 0, 7, 0)
            place = jnp.where(far == 0, row * 7, place)
            fetched_here = (chip_gap < 0) == (my_core == 0)
            tile = jnp.where(fetched_here, last_ref[groups + place], last_mate_ref[groups + place])
            tile = jnp.where(jnp.abs(chip_gap) == 2, beyond_ref[place], tile)
            tile = jnp.where(chip_gap == 0, coeffs_ref[place], tile).astype(F32)
            half = jnp.where(source >= 2, tile[8:], tile[:8])
            half = jnp.where(source & 1 == 1, half[:, 64:], half[:, :64])
            live = slot < coupling_count_ref[leaf]
            source_ref[leaf, slot * 8 : slot * 8 + 8, :] = jnp.where(live, half, 0.0)
    totals = [couple(leaf_coupling_ref[leaf], source_ref[leaf]) for leaf in range(4)]
    coarse_field = sum_groups(couple(coarse_coupling_ref[0], source_ref[4]))
    field_hi = coarse_field.astype(BF16).astype(F32)
    rest = coarse_field - field_hi
    field_mid = rest.astype(BF16).astype(F32)
    group = lax.broadcasted_iota(jnp.int32, (64, 128), 1) // 8
    parts = jnp.where(group == 2, rest - field_mid, 0.0)
    parts = jnp.where(group == 1, field_mid, jnp.where(group == 0, field_hi, parts)).astype(BF16)
    for leaf in range(4):
        totals[leaf] += jnp.dot(transfer_ref[leaf], parts, preferred_element_type=F32)
    local = sum_groups(jnp.concatenate(totals, axis=0)).T[:8]
    for leaf in range(4):
        mine = local[:, leaf * 64 : leaf * 64 + 64].astype(BF16)
        far_part = lax.dot_general(mine, basis_ref[leaf], NN, preferred_element_type=F32)
        span = slice(leaf * 256, leaf * 256 + 256)
        out_ref[:, span] = (near_ref[leaf] + far_part).astype(BF16)


VMEM = pl.BlockSpec(memory_space=pltpu.VMEM)
ANY = pl.BlockSpec(memory_space=pl.ANY)
SMEM = pl.BlockSpec(memory_space=pltpu.SMEM)
PARAMS = pltpu.CompilerParams(vmem_limit_bytes=16 * 2**20)


def near_call(cols, *operands):
    return pl.pallas_call(
        functools.partial(near_kernel, cols),
        out_shape=jax.ShapeDtypeStruct((4, 8, 256), F32),
        in_specs=[SMEM] * 2 + [VMEM] * 3,
        out_specs=VMEM,
        scratch_shapes=[pltpu.VMEM((4, 3, 32, 8, 128), F32)],
        compiler_params=PARAMS,
        name="near",
        cost_estimate=pl.CostEstimate(
            flops=4_000_000_000, bytes_accessed=1_200_000, transcendentals=0
        ),
    )(*operands)


def far_call(groups, cols, zs, *operands):
    return pl.pallas_call(
        functools.partial(far_kernel, groups, cols, zs),
        out_shape=jax.ShapeDtypeStruct((8, 1024), BF16),
        in_specs=[SMEM] * 5 + [VMEM] * 9,
        out_specs=VMEM,
        scratch_shapes=[pltpu.VMEM((5, 128, 64), F32)],
        compiler_params=PARAMS,
        name="far",
    )(*operands)


def per_device(
    xs,
    ys,
    zs,
    rhs,
    points,
    basis,
    transfer,
    leaf_coupling,
    coupling_list,
    coupling_count,
    coarse_coupling,
    coarse_list,
    coarse_count,
    owner,
    near_list,
    near_count,
):
    cols = ys * zs
    groups = xs * cols // 4
    half = zs // 2
    turned = [half, 0] + [z for near in range(1, half) for z in (near, zs - near)]
    basis = jnp.swapaxes(basis, 1, 2)

    blocks, cluster = pl.pallas_call(
        pack_kernel,
        out_shape=(
            jax.ShapeDtypeStruct((2, BLOCK, 16, 128), BF16),
            jax.ShapeDtypeStruct((zs, 4, 128), BF16),
        ),
        in_specs=[ANY] * 4,
        out_specs=(VMEM, VMEM),
        scratch_shapes=[
            pltpu.VMEM(rhs.shape, BF16),
            pltpu.VMEM(points.shape, F32),
            pltpu.VMEM(basis.shape, BF16),
            pltpu.VMEM(transfer.shape, BF16),
            pltpu.SemaphoreType.DMA((4,)),
        ],
        name="pack",
    )(rhs, points, basis, transfer)

    def along_col(step):
        pairs = []
        for core in range(2):
            for col in range(cols):
                source = col + step if core == 0 else col - step
                if 0 <= source < cols:
                    pairs.append((core * cols + source, core * cols + col))
        return pairs

    def along_x(step):
        pairs = []
        for x in range(xs):
            for core in range(2):
                source = x - step if core == 0 else x + step
                if 0 <= source < xs:
                    pairs.append((source * 2 + core, x * 2 + core))
        return pairs

    def coeffs_of(window):
        parts = [window[:, place : place + 1] for place in (9, 19, 29)]
        return jnp.concatenate(parts + [window[:, 30:]], axis=1).reshape(14, 16, 128)

    chip = lax.all_gather(blocks, "core", axis=0, tiled=False)
    first = lax.ppermute(chip, ("core", "y", "z"), along_col(1))[:, 0]
    chip, cluster = lax.optimization_barrier((chip, cluster))
    line = lax.all_to_all(
        cluster, "z", 0, 0, tiled=True, axis_index_groups=[turned]
    ).reshape(zs // 4, 16, 128)
    second = jnp.concatenate([chip[:, 0, 9:], first[:, 9:]], axis=1)
    second = lax.ppermute(second, ("core", "y", "z"), along_col(2))
    line = jnp.broadcast_to(line[None], (xs * ys,) + line.shape)
    same = lax.all_to_all(line, ("x", "y"), 0, 0, tiled=True).reshape(groups, 16, 128)

    window = jnp.concatenate(
        [blocks[0], first.reshape(2 * BLOCK, 16, 128), second.reshape(4, 16, 128)], axis=0
    )
    window = lax.all_gather(window, "core", axis=0, tiled=False)
    beside = lax.ppermute(window, ("x", "core"), along_x(1))
    coeffs = coeffs_of(window)
    beyond = lax.ppermute(coeffs, ("x", "core"), along_x(2))
    same, beside = lax.optimization_barrier((same, beside))
    last = jnp.concatenate([same, coeffs_of(beside)], axis=0)
    last, beside = lax.optimization_barrier((last, beside))
    near = near_call(cols, near_list, near_count, points, window, beside)
    last_mate = lax.ppermute(last, "core", [(0, 1), (1, 0)])

    return far_call(
        groups,
        cols,
        zs,
        coupling_list,
        coupling_count,
        coarse_list,
        coarse_count,
        owner,
        coeffs,
        last,
        last_mate,
        beyond,
        leaf_coupling,
        coarse_coupling,
        transfer,
        basis,
        near,
    )


def solution(mesh):
    rows, cols = mesh.devices.shape
    xs, ys = rows // 2, 4
    zs = cols // ys
    axes = ("x", "core", "y", "z")
    fine = Mesh(mesh.devices.reshape(xs, 2, ys, zs), axes)
    in_specs = (
        P(None, axes),
        P(None, axes),
        P(axes, None, None),
        P(axes, None, None),
        P(axes, None, None, None),
        P(axes, None),
        P(axes),
        P(axes, None, None, None),
        P(axes, None),
        P(axes),
        P(),
        P(axes, None),
        P(axes),
    )
    return jax.shard_map(
        functools.partial(per_device, xs, ys, zs),
        mesh=fine,
        in_specs=in_specs,
        out_specs=P(None, axes),
        check_vma=False,
    )
```

```python
import functools

import jax
import jax.numpy as jnp
from jax import lax
from jax.experimental import pallas as pl
from jax.experimental.pallas import tpu as pltpu
from jax.sharding import Mesh, PartitionSpec as P

FOUR_PI = 12.566370614359172
SOFTEN = 0.0025
F32 = jnp.float32
BF16 = jnp.bfloat16
NN = (((1,), (0,)), ((), ()))
NT = (((1,), (1,)), ((), ()))

BLOCK = 10


def fetch_all(sources, targets, done_ref):
    copies = [
        pltpu.make_async_copy(source, target, done_ref.at[place])
        for place, (source, target) in enumerate(zip(sources, targets))
    ]
    for copy in copies:
        copy.start()
    for copy in copies:
        copy.wait()


def pack_kernel(
    rhs_hbm,
    points_hbm,
    basis_hbm,
    transfer_hbm,
    copies_ref,
    cluster_ref,
    rhs_ref,
    points_ref,
    basis_ref,
    transfer_ref,
    done_ref,
):
    fetch_all(
        (rhs_hbm, points_hbm, basis_hbm, transfer_hbm),
        (rhs_ref, points_ref, basis_ref, transfer_ref),
        done_ref,
    )
    block_ref = copies_ref.at[0]
    points = points_ref[...]
    part_hi = points.astype(BF16).astype(F32)
    rest = points - part_hi
    part_mid = rest.astype(BF16).astype(F32)
    part_lo = rest - part_mid
    parts = jnp.concatenate([part_hi, part_mid, part_lo[:2]], axis=0)
    cluster = jnp.zeros((8, 64), F32)
    coeffs = []
    last_rows = []
    for leaf in range(4):
        low = slice(leaf * 256, leaf * 256 + 128)
        high = slice(leaf * 256 + 128, leaf * 256 + 256)
        sides = rhs_ref[:, leaf * 256 : leaf * 256 + 256]
        coeff = lax.dot_general(sides, basis_ref[leaf], NT, preferred_element_type=F32)
        coeff = coeff.astype(BF16)
        cluster = cluster + jnp.dot(coeff, transfer_ref[leaf], preferred_element_type=F32)
        coeffs.append(coeff.astype(F32))
        wide = sides.astype(F32)
        block_ref[leaf] = jnp.concatenate([wide[:, :128], wide[:, 128:]], axis=0).astype(BF16)
        block_ref[4 + leaf] = jnp.concatenate([parts[:, low], parts[:, high]], axis=0).astype(BF16)
        last_rows += [part_lo[2:3, low], part_lo[2:3, high]]
    block_ref[8] = jnp.concatenate(last_rows + [jnp.zeros((8, 128), F32)], axis=0).astype(BF16)
    block_ref[9] = jnp.concatenate(
        [jnp.concatenate(coeffs[:2], axis=1), jnp.concatenate(coeffs[2:], axis=1)], axis=0
    ).astype(BF16)
    copies_ref[1] = block_ref[...]
    packed = jnp.concatenate([cluster[:4], cluster[4:]], axis=1).astype(BF16)
    cluster_ref[...] = jnp.broadcast_to(packed[None], cluster_ref.shape)


def locate(leaf_id, cols):
    device = lax.shift_right_logical(leaf_id, 2)
    row = lax.shift_right_logical(device, cols.bit_length() - 1)
    chip_gap = (row >> 1) - lax.axis_index("x")
    gap = (device & (cols - 1)) - lax.axis_index(("y", "z"))
    return chip_gap, row & 1, gap, leaf_id & 3


def near_kernel(
    base_leaf,
    cols,
    list_ref,
    count_ref,
    points_ref,
    window_ref,
    beside_ref,
    near_ref,
    wide_ref,
):
    scale = F32(FOUR_PI * FOUR_PI)
    floor = F32(FOUR_PI * FOUR_PI * SOFTEN)
    row_ids = lax.broadcasted_iota(jnp.int32, (8, 128), 0)

    def source_of(leaf, slot):
        chip_gap, row, gap, source = locate(list_ref[leaf, slot], cols)
        holder = jnp.where(gap == 0, row, jnp.where(gap > 0, 0, 1))
        base = jnp.where(gap == 0, 0, BLOCK + row * BLOCK)

        def fetch(place):
            here = window_ref[holder, base + place]
            return jnp.where(chip_gap == 0, here, beside_ref[holder, base + place]).astype(F32)

        sides = fetch(source)
        sides = jnp.concatenate([sides[:8], sides[8:]], axis=1)
        sides = jnp.where(slot < count_ref[leaf], sides, 0.0).astype(BF16)
        parts = fetch(4 + source)
        last = fetch(8)[:8]
        halves = []
        for half in range(2):
            part = parts[half * 8 : half * 8 + 8]
            tail = jnp.sum(
                jnp.where(row_ids == source * 2 + half, last, 0.0), axis=0, keepdims=True
            )
            place = (
                part[0:1] + part[3:4] + part[6:7],
                part[1:2] + part[4:5] + part[7:8],
                part[2:3] + part[5:6] + tail,
            )
            halves.append([jnp.broadcast_to(line, (8, 128)) for line in place])
        return sides, halves

    for leaf in range(2):
        span = slice((base_leaf + leaf) * 256, (base_leaf + leaf) * 256 + 256)
        own = points_ref[:, span]
        own = jnp.concatenate([own, jnp.zeros((5, 256), F32)], axis=0).T
        for axis in range(3):
            wide = jnp.broadcast_to(own[:, axis : axis + 1], (256, 128))
            wide_ref[leaf, axis] = wide.reshape(32, 8, 128)

    def leaf_step(leaf, carry):
        total = jnp.zeros((8, 256), F32)
        for slot in range(8):
            sides, halves = source_of(base_leaf + leaf, slot)
            bands = []
            for band in range(0, 32, 8):
                tiles = []
                target = [wide_ref[leaf, axis, band : band + 8] for axis in range(3)]
                for place in halves:
                    first = target[0] - place[0]
                    second = target[1] - place[1]
                    third = target[2] - place[2]
                    dist_sq = first * first + second * second + third * third
                    inverse = lax.rsqrt(dist_sq * scale + floor)
                    tiles.append(inverse.reshape(64, 128).astype(BF16))
                bands.append(jnp.concatenate(tiles, axis=1))
            tile = jnp.concatenate(bands, axis=0)
            total += lax.dot_general(sides, tile, NT, preferred_element_type=F32)
        near_ref[leaf] = total
        return carry

    lax.fori_loop(0, 2, leaf_step, 0, unroll=2)


def couple(matrices, sources):
    slots = matrices.shape[0]
    products = lax.dot_general(
        matrices.reshape(slots * 64, 64), sources.astype(BF16), NT, preferred_element_type=F32
    )
    group = lax.broadcasted_iota(jnp.int32, (64, 128), 1) // 8
    total = products[:64]
    for slot in range(1, slots):
        total = jnp.where(group == slot, products[slot * 64 : slot * 64 + 64], total)
    return total


def sum_groups(total):
    for shift in (64, 32, 16, 8):
        total = total + pltpu.roll(total, shift, 1)
    return total


def far_kernel(
    groups,
    cols,
    zs,
    coupling_list_ref,
    coupling_count_ref,
    coarse_list_ref,
    coarse_count_ref,
    owner_ref,
    coeffs_ref,
    last_ref,
    last_mate_ref,
    beyond_ref,
    leaf_coupling_ref,
    coarse_coupling_ref,
    transfer_ref,
    basis_ref,
    near_low_ref,
    near_high_ref,
    out_ref,
    source_ref,
):
    my_core = lax.axis_index("core")
    for slot in range(16):
        device = owner_ref[coarse_list_ref[0, slot]]
        row = lax.shift_right_logical(device, cols.bit_length() - 1)
        col = device & (cols - 1)
        z = col & (zs - 1)
        order = jnp.where(z < zs // 2, z * 2, (zs - z) * 2 + 1)
        order = jnp.where(z == 0, 1, jnp.where(z == zs // 2, 0, order))
        tile_id = (row >> 1) * (cols // 4) + ((col - z + order) >> 2)
        mine = (row & 1) == my_core
        tile = jnp.where(mine, last_ref[tile_id], last_mate_ref[tile_id]).astype(F32)
        place = order & 3
        picked = tile[0:4]
        for step in range(1, 4):
            picked = jnp.where(place == step, tile[step * 4 : step * 4 + 4], picked)
        picked = jnp.where(slot < coarse_count_ref[0], picked, 0.0)
        source_ref[4, slot * 8 : slot * 8 + 8, :] = jnp.concatenate(
            [picked[:, :64], picked[:, 64:]], axis=0
        )
    for leaf in range(4):
        for slot in range(16):
            chip_gap, row, gap, source = locate(coupling_list_ref[leaf, slot], cols)
            far = jnp.abs(gap)
            place = jnp.where(far == 1, 1 + row, 1 + row * 2 + far) + jnp.where(gap < 0, 7, 0)
            place = jnp.where(far == 0, row * 7, place)
            fetched_here = (chip_gap < 0) == (my_core == 0)
            tile = jnp.where(fetched_here, last_ref[groups + place], last_mate_ref[groups + place])
            tile = jnp.where(jnp.abs(chip_gap) == 2, beyond_ref[place], tile)
            tile = jnp.where(chip_gap == 0, coeffs_ref[place], tile).astype(F32)
            half = jnp.where(source >= 2, tile[8:], tile[:8])
            half = jnp.where(source & 1 == 1, half[:, 64:], half[:, :64])
            live = slot < coupling_count_ref[leaf]
            source_ref[leaf, slot * 8 : slot * 8 + 8, :] = jnp.where(live, half, 0.0)
    totals = [couple(leaf_coupling_ref[leaf], source_ref[leaf]) for leaf in range(4)]
    coarse_field = sum_groups(couple(coarse_coupling_ref[0], source_ref[4]))
    field_hi = coarse_field.astype(BF16).astype(F32)
    rest = coarse_field - field_hi
    field_mid = rest.astype(BF16).astype(F32)
    group = lax.broadcasted_iota(jnp.int32, (64, 128), 1) // 8
    parts = jnp.where(group == 2, rest - field_mid, 0.0)
    parts = jnp.where(group == 1, field_mid, jnp.where(group == 0, field_hi, parts)).astype(BF16)
    for leaf in range(4):
        totals[leaf] += jnp.dot(transfer_ref[leaf], parts, preferred_element_type=F32)
    local = sum_groups(jnp.concatenate(totals, axis=0)).T[:8]
    for leaf in range(4):
        mine = local[:, leaf * 64 : leaf * 64 + 64].astype(BF16)
        far_part = lax.dot_general(mine, basis_ref[leaf], NN, preferred_element_type=F32)
        span = slice(leaf * 256, leaf * 256 + 256)
        near_part = near_low_ref[leaf] if leaf < 2 else near_high_ref[leaf - 2]
        out_ref[:, span] = (near_part + far_part).astype(BF16)


VMEM = pl.BlockSpec(memory_space=pltpu.VMEM)
ANY = pl.BlockSpec(memory_space=pl.ANY)
SMEM = pl.BlockSpec(memory_space=pltpu.SMEM)
PARAMS = pltpu.CompilerParams(vmem_limit_bytes=16 * 2**20)


def near_call(base_leaf, cols, *operands):
    return pl.pallas_call(
        functools.partial(near_kernel, base_leaf, cols),
        out_shape=jax.ShapeDtypeStruct((2, 8, 256), F32),
        in_specs=[SMEM] * 2 + [VMEM] * 3,
        out_specs=VMEM,
        scratch_shapes=[pltpu.VMEM((2, 3, 32, 8, 128), F32)],
        compiler_params=PARAMS,
        name=f"near{base_leaf}",
        cost_estimate=pl.CostEstimate(
            flops=100_000_000, bytes_accessed=1_200_000, transcendentals=0
        ),
    )(*operands)


def far_call(groups, cols, zs, *operands):
    return pl.pallas_call(
        functools.partial(far_kernel, groups, cols, zs),
        out_shape=jax.ShapeDtypeStruct((8, 1024), BF16),
        in_specs=[SMEM] * 5 + [VMEM] * 10,
        out_specs=VMEM,
        scratch_shapes=[pltpu.VMEM((5, 128, 64), F32)],
        compiler_params=PARAMS,
        name="far",
    )(*operands)


def per_device(
    xs,
    ys,
    zs,
    rhs,
    points,
    basis,
    transfer,
    leaf_coupling,
    coupling_list,
    coupling_count,
    coarse_coupling,
    coarse_list,
    coarse_count,
    owner,
    near_list,
    near_count,
):
    cols = ys * zs
    groups = xs * cols // 4
    half = zs // 2
    turned = [half, 0] + [z for near in range(1, half) for z in (near, zs - near)]
    basis = jnp.swapaxes(basis, 1, 2)

    blocks, cluster = pl.pallas_call(
        pack_kernel,
        out_shape=(
            jax.ShapeDtypeStruct((2, BLOCK, 16, 128), BF16),
            jax.ShapeDtypeStruct((zs, 4, 128), BF16),
        ),
        in_specs=[ANY] * 4,
        out_specs=(VMEM, VMEM),
        scratch_shapes=[
            pltpu.VMEM(rhs.shape, BF16),
            pltpu.VMEM(points.shape, F32),
            pltpu.VMEM(basis.shape, BF16),
            pltpu.VMEM(transfer.shape, BF16),
            pltpu.SemaphoreType.DMA((4,)),
        ],
        name="pack",
    )(rhs, points, basis, transfer)

    def along_col(step):
        pairs = []
        for core in range(2):
            for col in range(cols):
                source = col + step if core == 0 else col - step
                if 0 <= source < cols:
                    pairs.append((core * cols + source, core * cols + col))
        return pairs

    def along_x(step):
        pairs = []
        for x in range(xs):
            for core in range(2):
                source = x - step if core == 0 else x + step
                if 0 <= source < xs:
                    pairs.append((source * 2 + core, x * 2 + core))
        return pairs

    def coeffs_of(window):
        parts = [window[:, place : place + 1] for place in (9, 19, 29)]
        return jnp.concatenate(parts + [window[:, 30:]], axis=1).reshape(14, 16, 128)

    chip = lax.all_gather(blocks, "core", axis=0, tiled=False)
    first = lax.ppermute(chip, ("core", "y", "z"), along_col(1))[:, 0]
    chip, cluster = lax.optimization_barrier((chip, cluster))
    line = lax.all_to_all(
        cluster, "z", 0, 0, tiled=True, axis_index_groups=[turned]
    ).reshape(zs // 4, 16, 128)
    second = jnp.concatenate([chip[:, 0, 9:], first[:, 9:]], axis=1)
    second = lax.ppermute(second, ("core", "y", "z"), along_col(2))
    first, line = lax.optimization_barrier((first, line))
    line = jnp.broadcast_to(line[None], (xs * ys,) + line.shape)
    same = lax.all_to_all(line, ("x", "y"), 0, 0, tiled=True).reshape(groups, 16, 128)

    window = jnp.concatenate(
        [blocks[0], first.reshape(2 * BLOCK, 16, 128), second.reshape(4, 16, 128)], axis=0
    )
    window = lax.all_gather(window, "core", axis=0, tiled=False)
    beside = lax.ppermute(window, ("x", "core"), along_x(1))
    coeffs = coeffs_of(window)
    beyond = lax.ppermute(coeffs, ("x", "core"), along_x(2))
    near_low = near_call(0, cols, near_list, near_count, points, window, beside)
    same, beside, beyond, near_low = lax.optimization_barrier((same, beside, beyond, near_low))
    last = jnp.concatenate([same, coeffs_of(beside)], axis=0)
    last, beside = lax.optimization_barrier((last, beside))
    near_high = near_call(2, cols, near_list, near_count, points, window, beside)
    last_mate = lax.ppermute(last, "core", [(0, 1), (1, 0)])

    return far_call(
        groups,
        cols,
        zs,
        coupling_list,
        coupling_count,
        coarse_list,
        coarse_count,
        owner,
        coeffs,
        last,
        last_mate,
        beyond,
        leaf_coupling,
        coarse_coupling,
        transfer,
        basis,
        near_low,
        near_high,
    )


def solution(mesh):
    rows, cols = mesh.devices.shape
    xs, ys = rows // 2, 4
    zs = cols // ys
    axes = ("x", "core", "y", "z")
    fine = Mesh(mesh.devices.reshape(xs, 2, ys, zs), axes)
    in_specs = (
        P(None, axes),
        P(None, axes),
        P(axes, None, None),
        P(axes, None, None),
        P(axes, None, None, None),
        P(axes, None),
        P(axes),
        P(axes, None, None, None),
        P(axes, None),
        P(axes),
        P(),
        P(axes, None),
        P(axes),
    )
    return jax.shard_map(
        functools.partial(per_device, xs, ys, zs),
        mesh=fine,
        in_specs=in_specs,
        out_specs=P(None, axes),
        check_vma=False,
    )
```

```python
import functools

import jax
import jax.numpy as jnp
from jax import lax
from jax.experimental import pallas as pl
from jax.experimental.pallas import tpu as pltpu
from jax.sharding import Mesh, PartitionSpec as P

FOUR_PI = 12.566370614359172
SOFTEN = 0.0025
F32 = jnp.float32
BF16 = jnp.bfloat16
NN = (((1,), (0,)), ((), ()))
NT = (((1,), (1,)), ((), ()))

BLOCK = 10


def fetch_all(sources, targets, done_ref):
    copies = [
        pltpu.make_async_copy(source, target, done_ref.at[place])
        for place, (source, target) in enumerate(zip(sources, targets))
    ]
    for copy in copies:
        copy.start()
    for copy in copies:
        copy.wait()


def pack_kernel(
    rhs_ref,
    points_hbm,
    basis_hbm,
    transfer_hbm,
    copies_ref,
    cluster_ref,
    points_ref,
    basis_ref,
    transfer_ref,
    done_ref,
):
    fetch_all(
        (points_hbm, basis_hbm, transfer_hbm),
        (points_ref, basis_ref, transfer_ref),
        done_ref,
    )
    block_ref = copies_ref.at[0]
    points = points_ref[...]
    part_hi = points.astype(BF16).astype(F32)
    rest = points - part_hi
    part_mid = rest.astype(BF16).astype(F32)
    part_lo = rest - part_mid
    parts = jnp.concatenate([part_hi, part_mid, part_lo[:2]], axis=0)
    cluster = jnp.zeros((8, 64), F32)
    coeffs = []
    last_rows = []
    for leaf in range(4):
        low = slice(leaf * 256, leaf * 256 + 128)
        high = slice(leaf * 256 + 128, leaf * 256 + 256)
        sides = rhs_ref[:, leaf * 256 : leaf * 256 + 256]
        coeff = lax.dot_general(sides, basis_ref[leaf], NT, preferred_element_type=F32)
        coeff = coeff.astype(BF16)
        cluster = cluster + jnp.dot(coeff, transfer_ref[leaf], preferred_element_type=F32)
        coeffs.append(coeff.astype(F32))
        wide = sides.astype(F32)
        block_ref[leaf] = jnp.concatenate([wide[:, :128], wide[:, 128:]], axis=0).astype(BF16)
        block_ref[4 + leaf] = jnp.concatenate([parts[:, low], parts[:, high]], axis=0).astype(BF16)
        last_rows += [part_lo[2:3, low], part_lo[2:3, high]]
    block_ref[8] = jnp.concatenate(last_rows + [jnp.zeros((8, 128), F32)], axis=0).astype(BF16)
    block_ref[9] = jnp.concatenate(
        [jnp.concatenate(coeffs[:2], axis=1), jnp.concatenate(coeffs[2:], axis=1)], axis=0
    ).astype(BF16)
    copies_ref[1] = block_ref[...]
    packed = jnp.concatenate([cluster[:4], cluster[4:]], axis=1).astype(BF16)
    cluster_ref[...] = jnp.broadcast_to(packed[None], cluster_ref.shape)


def locate(leaf_id, cols):
    device = lax.shift_right_logical(leaf_id, 2)
    row = lax.shift_right_logical(device, cols.bit_length() - 1)
    chip_gap = (row >> 1) - lax.axis_index("x")
    gap = (device & (cols - 1)) - lax.axis_index(("y", "z"))
    return chip_gap, row & 1, gap, leaf_id & 3


def near_kernel(
    base_leaf,
    cols,
    list_ref,
    count_ref,
    points_ref,
    window_ref,
    beside_ref,
    near_ref,
    wide_ref,
):
    scale = F32(FOUR_PI * FOUR_PI)
    floor = F32(FOUR_PI * FOUR_PI * SOFTEN)
    row_ids = lax.broadcasted_iota(jnp.int32, (8, 128), 0)

    def source_of(leaf, slot):
        chip_gap, row, gap, source = locate(list_ref[leaf, slot], cols)
        holder = jnp.where(gap == 0, row, jnp.where(gap > 0, 0, 1))
        base = jnp.where(gap == 0, 0, BLOCK + row * BLOCK)

        def fetch(place):
            here = window_ref[holder, base + place]
            return jnp.where(chip_gap == 0, here, beside_ref[holder, base + place]).astype(F32)

        sides = fetch(source)
        sides = jnp.concatenate([sides[:8], sides[8:]], axis=1)
        sides = jnp.where(slot < count_ref[leaf], sides, 0.0).astype(BF16)
        parts = fetch(4 + source)
        last = fetch(8)[:8]
        halves = []
        for half in range(2):
            part = parts[half * 8 : half * 8 + 8]
            tail = jnp.sum(
                jnp.where(row_ids == source * 2 + half, last, 0.0), axis=0, keepdims=True
            )
            place = (
                part[0:1] + part[3:4] + part[6:7],
                part[1:2] + part[4:5] + part[7:8],
                part[2:3] + part[5:6] + tail,
            )
            halves.append([jnp.broadcast_to(line, (8, 128)) for line in place])
        return sides, halves

    for leaf in range(2):
        span = slice((base_leaf + leaf) * 256, (base_leaf + leaf) * 256 + 256)
        own = points_ref[:, span]
        own = jnp.concatenate([own, jnp.zeros((5, 256), F32)], axis=0).T
        for axis in range(3):
            wide = jnp.broadcast_to(own[:, axis : axis + 1], (256, 128))
            wide_ref[leaf, axis] = wide.reshape(32, 8, 128)

    def leaf_step(leaf, carry):
        total = jnp.zeros((8, 256), F32)
        for slot in range(8):
            sides, halves = source_of(base_leaf + leaf, slot)
            bands = []
            for band in range(0, 32, 8):
                tiles = []
                target = [wide_ref[leaf, axis, band : band + 8] for axis in range(3)]
                for place in halves:
                    first = target[0] - place[0]
                    second = target[1] - place[1]
                    third = target[2] - place[2]
                    dist_sq = first * first + second * second + third * third
                    inverse = lax.rsqrt(dist_sq * scale + floor)
                    tiles.append(inverse.reshape(64, 128).astype(BF16))
                bands.append(jnp.concatenate(tiles, axis=1))
            tile = jnp.concatenate(bands, axis=0)
            total += lax.dot_general(sides, tile, NT, preferred_element_type=F32)
        near_ref[leaf] = total
        return carry

    lax.fori_loop(0, 2, leaf_step, 0, unroll=2)


def couple(matrices, sources):
    slots = matrices.shape[0]
    products = lax.dot_general(
        matrices.reshape(slots * 64, 64), sources.astype(BF16), NT, preferred_element_type=F32
    )
    group = lax.broadcasted_iota(jnp.int32, (64, 128), 1) // 8
    total = products[:64]
    for slot in range(1, slots):
        total = jnp.where(group == slot, products[slot * 64 : slot * 64 + 64], total)
    return total


def sum_groups(total):
    for shift in (64, 32, 16, 8):
        total = total + pltpu.roll(total, shift, 1)
    return total


def far_kernel(
    groups,
    cols,
    zs,
    coupling_list_ref,
    coupling_count_ref,
    coarse_list_ref,
    coarse_count_ref,
    owner_ref,
    coeffs_ref,
    last_ref,
    last_mate_ref,
    beyond_ref,
    leaf_coupling_ref,
    coarse_coupling_ref,
    transfer_ref,
    basis_ref,
    near_low_ref,
    near_high_ref,
    out_ref,
    source_ref,
):
    my_core = lax.axis_index("core")
    for slot in range(16):
        device = owner_ref[coarse_list_ref[0, slot]]
        row = lax.shift_right_logical(device, cols.bit_length() - 1)
        col = device & (cols - 1)
        z = col & (zs - 1)
        order = jnp.where(z < zs // 2, z * 2, (zs - z) * 2 + 1)
        order = jnp.where(z == 0, 1, jnp.where(z == zs // 2, 0, order))
        tile_id = (row >> 1) * (cols // 4) + ((col - z + order) >> 2)
        mine = (row & 1) == my_core
        tile = jnp.where(mine, last_ref[tile_id], last_mate_ref[tile_id]).astype(F32)
        place = order & 3
        picked = tile[0:4]
        for step in range(1, 4):
            picked = jnp.where(place == step, tile[step * 4 : step * 4 + 4], picked)
        picked = jnp.where(slot < coarse_count_ref[0], picked, 0.0)
        source_ref[4, slot * 8 : slot * 8 + 8, :] = jnp.concatenate(
            [picked[:, :64], picked[:, 64:]], axis=0
        )
    for leaf in range(4):
        for slot in range(16):
            chip_gap, row, gap, source = locate(coupling_list_ref[leaf, slot], cols)
            far = jnp.abs(gap)
            place = jnp.where(far == 1, 1 + row, 1 + row * 2 + far) + jnp.where(gap < 0, 7, 0)
            place = jnp.where(far == 0, row * 7, place)
            fetched_here = (chip_gap < 0) == (my_core == 0)
            tile = jnp.where(fetched_here, last_ref[groups + place], last_mate_ref[groups + place])
            tile = jnp.where(jnp.abs(chip_gap) == 2, beyond_ref[place], tile)
            tile = jnp.where(chip_gap == 0, coeffs_ref[place], tile).astype(F32)
            half = jnp.where(source >= 2, tile[8:], tile[:8])
            half = jnp.where(source & 1 == 1, half[:, 64:], half[:, :64])
            live = slot < coupling_count_ref[leaf]
            source_ref[leaf, slot * 8 : slot * 8 + 8, :] = jnp.where(live, half, 0.0)
    totals = [couple(leaf_coupling_ref[leaf], source_ref[leaf]) for leaf in range(4)]
    coarse_field = sum_groups(couple(coarse_coupling_ref[0], source_ref[4]))
    field_hi = coarse_field.astype(BF16).astype(F32)
    rest = coarse_field - field_hi
    field_mid = rest.astype(BF16).astype(F32)
    group = lax.broadcasted_iota(jnp.int32, (64, 128), 1) // 8
    parts = jnp.where(group == 2, rest - field_mid, 0.0)
    parts = jnp.where(group == 1, field_mid, jnp.where(group == 0, field_hi, parts)).astype(BF16)
    for leaf in range(4):
        totals[leaf] += jnp.dot(transfer_ref[leaf], parts, preferred_element_type=F32)
    local = sum_groups(jnp.concatenate(totals, axis=0)).T[:8]
    for leaf in range(4):
        mine = local[:, leaf * 64 : leaf * 64 + 64].astype(BF16)
        far_part = lax.dot_general(mine, basis_ref[leaf], NN, preferred_element_type=F32)
        span = slice(leaf * 256, leaf * 256 + 256)
        near_part = near_low_ref[leaf] if leaf < 2 else near_high_ref[leaf - 2]
        out_ref[:, span] = (near_part + far_part).astype(BF16)


VMEM = pl.BlockSpec(memory_space=pltpu.VMEM)
ANY = pl.BlockSpec(memory_space=pl.ANY)
SMEM = pl.BlockSpec(memory_space=pltpu.SMEM)
PARAMS = pltpu.CompilerParams(vmem_limit_bytes=16 * 2**20)


def near_call(base_leaf, cols, *operands):
    return pl.pallas_call(
        functools.partial(near_kernel, base_leaf, cols),
        out_shape=jax.ShapeDtypeStruct((2, 8, 256), F32),
        in_specs=[SMEM] * 2 + [VMEM] * 3,
        out_specs=VMEM,
        scratch_shapes=[pltpu.VMEM((2, 3, 32, 8, 128), F32)],
        compiler_params=PARAMS,
        name=f"near{base_leaf}",
        cost_estimate=pl.CostEstimate(
            flops=100_000_000, bytes_accessed=1_200_000, transcendentals=0
        ),
    )(*operands)


def far_call(groups, cols, zs, *operands):
    return pl.pallas_call(
        functools.partial(far_kernel, groups, cols, zs),
        out_shape=jax.ShapeDtypeStruct((8, 1024), BF16),
        in_specs=[SMEM] * 5 + [VMEM] * 10,
        out_specs=VMEM,
        scratch_shapes=[pltpu.VMEM((5, 128, 64), F32)],
        compiler_params=PARAMS,
        name="far",
    )(*operands)


def per_device(
    xs,
    ys,
    zs,
    rhs,
    points,
    basis,
    transfer,
    leaf_coupling,
    coupling_list,
    coupling_count,
    coarse_coupling,
    coarse_list,
    coarse_count,
    owner,
    near_list,
    near_count,
):
    cols = ys * zs
    groups = xs * cols // 4
    half = zs // 2
    turned = [half, 0] + [z for near in range(1, half) for z in (near, zs - near)]
    basis = jnp.swapaxes(basis, 1, 2)

    blocks, cluster = pl.pallas_call(
        pack_kernel,
        out_shape=(
            jax.ShapeDtypeStruct((2, BLOCK, 16, 128), BF16),
            jax.ShapeDtypeStruct((zs, 4, 128), BF16),
        ),
        in_specs=[VMEM] + [ANY] * 3,
        out_specs=(VMEM, VMEM),
        scratch_shapes=[
            pltpu.VMEM(points.shape, F32),
            pltpu.VMEM(basis.shape, BF16),
            pltpu.VMEM(transfer.shape, BF16),
            pltpu.SemaphoreType.DMA((3,)),
        ],
        name="pack",
    )(rhs, points, basis, transfer)

    def along_col(step):
        pairs = []
        for core in range(2):
            for col in range(cols):
                source = col + step if core == 0 else col - step
                if 0 <= source < cols:
                    pairs.append((core * cols + source, core * cols + col))
        return pairs

    def along_x(step):
        pairs = []
        for x in range(xs):
            for core in range(2):
                source = x - step if core == 0 else x + step
                if 0 <= source < xs:
                    pairs.append((source * 2 + core, x * 2 + core))
        return pairs

    def coeffs_of(window):
        parts = [window[:, place : place + 1] for place in (9, 19, 29)]
        return jnp.concatenate(parts + [window[:, 30:]], axis=1).reshape(14, 16, 128)

    chip = lax.all_gather(blocks, "core", axis=0, tiled=False)
    first = lax.ppermute(chip, ("core", "y", "z"), along_col(1))[:, 0]
    chip, cluster = lax.optimization_barrier((chip, cluster))
    line = lax.all_to_all(
        cluster, "z", 0, 0, tiled=True, axis_index_groups=[turned]
    ).reshape(zs // 4, 16, 128)
    second = jnp.concatenate([chip[:, 0, 9:], first[:, 9:]], axis=1)
    second = lax.ppermute(second, ("core", "y", "z"), along_col(2))
    first, line = lax.optimization_barrier((first, line))
    line = jnp.broadcast_to(line[None], (xs * ys,) + line.shape)
    same = lax.all_to_all(line, ("x", "y"), 0, 0, tiled=True).reshape(groups, 16, 128)

    window = jnp.concatenate(
        [blocks[0], first.reshape(2 * BLOCK, 16, 128), second.reshape(4, 16, 128)], axis=0
    )
    window = lax.all_gather(window, "core", axis=0, tiled=False)
    beside = lax.ppermute(window, ("x", "core"), along_x(1))
    coeffs = coeffs_of(window)
    beyond = lax.ppermute(coeffs, ("x", "core"), along_x(2))
    near_low = near_call(0, cols, near_list, near_count, points, window, beside)
    same, beside, beyond, near_low = lax.optimization_barrier((same, beside, beyond, near_low))
    last = jnp.concatenate([same, coeffs_of(beside)], axis=0)
    last, beside = lax.optimization_barrier((last, beside))
    near_high = near_call(2, cols, near_list, near_count, points, window, beside)
    last_mate = lax.ppermute(last, "core", [(0, 1), (1, 0)])

    return far_call(
        groups,
        cols,
        zs,
        coupling_list,
        coupling_count,
        coarse_list,
        coarse_count,
        owner,
        coeffs,
        last,
        last_mate,
        beyond,
        leaf_coupling,
        coarse_coupling,
        transfer,
        basis,
        near_low,
        near_high,
    )


def solution(mesh):
    rows, cols = mesh.devices.shape
    xs, ys = rows // 2, 4
    zs = cols // ys
    axes = ("x", "core", "y", "z")
    fine = Mesh(mesh.devices.reshape(xs, 2, ys, zs), axes)
    in_specs = (
        P(None, axes),
        P(None, axes),
        P(axes, None, None),
        P(axes, None, None),
        P(axes, None, None, None),
        P(axes, None),
        P(axes),
        P(axes, None, None, None),
        P(axes, None),
        P(axes),
        P(),
        P(axes, None),
        P(axes),
    )
    return jax.shard_map(
        functools.partial(per_device, xs, ys, zs),
        mesh=fine,
        in_specs=in_specs,
        out_specs=P(None, axes),
        check_vma=False,
    )
```

```python
import functools

import jax
import jax.numpy as jnp
from jax import lax
from jax.experimental import pallas as pl
from jax.experimental.pallas import tpu as pltpu
from jax.sharding import Mesh, PartitionSpec as P

FOUR_PI = 12.566370614359172
SOFTEN = 0.0025
F32 = jnp.float32
BF16 = jnp.bfloat16
NN = (((1,), (0,)), ((), ()))
NT = (((1,), (1,)), ((), ()))

BLOCK = 10


def pack_kernel(
    rhs_ref,
    points_hbm,
    basis_hbm,
    transfer_hbm,
    copies_ref,
    cluster_ref,
    points_ref,
    basis_ref,
    transfer_ref,
    done_ref,
):
    pairs = ((points_hbm, points_ref), (basis_hbm, basis_ref), (transfer_hbm, transfer_ref))
    copies = [
        pltpu.make_async_copy(source, target, done_ref.at[place])
        for place, (source, target) in enumerate(pairs)
    ]
    for copy in copies:
        copy.start()
    block_ref = copies_ref.at[0]
    copies[0].wait()
    points = points_ref[...]
    part_hi = points.astype(BF16).astype(F32)
    rest = points - part_hi
    part_mid = rest.astype(BF16).astype(F32)
    part_lo = rest - part_mid
    parts = jnp.concatenate([part_hi, part_mid, part_lo[:2]], axis=0)
    last_rows = []
    for leaf in range(4):
        low = slice(leaf * 256, leaf * 256 + 128)
        high = slice(leaf * 256 + 128, leaf * 256 + 256)
        wide = rhs_ref[:, leaf * 256 : leaf * 256 + 256].astype(F32)
        block_ref[leaf] = jnp.concatenate([wide[:, :128], wide[:, 128:]], axis=0).astype(BF16)
        block_ref[4 + leaf] = jnp.concatenate([parts[:, low], parts[:, high]], axis=0).astype(BF16)
        last_rows += [part_lo[2:3, low], part_lo[2:3, high]]
    block_ref[8] = jnp.concatenate(last_rows + [jnp.zeros((8, 128), F32)], axis=0).astype(BF16)
    copies[1].wait()
    coeffs = []
    for leaf in range(4):
        sides = rhs_ref[:, leaf * 256 : leaf * 256 + 256]
        coeff = lax.dot_general(sides, basis_ref[leaf], NT, preferred_element_type=F32)
        coeffs.append(coeff.astype(BF16).astype(F32))
    block_ref[9] = jnp.concatenate(
        [jnp.concatenate(coeffs[:2], axis=1), jnp.concatenate(coeffs[2:], axis=1)], axis=0
    ).astype(BF16)
    copies_ref[1] = block_ref[...]
    copies[2].wait()
    cluster = jnp.zeros((8, 64), F32)
    for leaf in range(4):
        coeff = coeffs[leaf].astype(BF16)
        cluster = cluster + jnp.dot(coeff, transfer_ref[leaf], preferred_element_type=F32)
    packed = jnp.concatenate([cluster[:4], cluster[4:]], axis=1).astype(BF16)
    cluster_ref[...] = jnp.broadcast_to(packed[None], cluster_ref.shape)


def locate(leaf_id, cols):
    device = lax.shift_right_logical(leaf_id, 2)
    row = lax.shift_right_logical(device, cols.bit_length() - 1)
    chip_gap = (row >> 1) - lax.axis_index("x")
    gap = (device & (cols - 1)) - lax.axis_index(("y", "z"))
    return chip_gap, row & 1, gap, leaf_id & 3


def near_kernel(
    base_leaf,
    cols,
    list_ref,
    count_ref,
    points_ref,
    window_ref,
    beside_ref,
    near_ref,
    wide_ref,
):
    scale = F32(FOUR_PI * FOUR_PI)
    floor = F32(FOUR_PI * FOUR_PI * SOFTEN)
    row_ids = lax.broadcasted_iota(jnp.int32, (8, 128), 0)

    def source_of(leaf, slot):
        chip_gap, row, gap, source = locate(list_ref[leaf, slot], cols)
        holder = jnp.where(gap == 0, row, jnp.where(gap > 0, 0, 1))
        base = jnp.where(gap == 0, 0, BLOCK + row * BLOCK)

        def fetch(place):
            here = window_ref[holder, base + place]
            return jnp.where(chip_gap == 0, here, beside_ref[holder, base + place]).astype(F32)

        sides = fetch(source)
        sides = jnp.concatenate([sides[:8], sides[8:]], axis=1)
        sides = jnp.where(slot < count_ref[leaf], sides, 0.0).astype(BF16)
        parts = fetch(4 + source)
        last = fetch(8)[:8]
        halves = []
        for half in range(2):
            part = parts[half * 8 : half * 8 + 8]
            tail = jnp.sum(
                jnp.where(row_ids == source * 2 + half, last, 0.0), axis=0, keepdims=True
            )
            place = (
                part[0:1] + part[3:4] + part[6:7],
                part[1:2] + part[4:5] + part[7:8],
                part[2:3] + part[5:6] + tail,
            )
            halves.append([jnp.broadcast_to(line, (8, 128)) for line in place])
        return sides, halves

    for leaf in range(2):
        span = slice((base_leaf + leaf) * 256, (base_leaf + leaf) * 256 + 256)
        own = points_ref[:, span]
        own = jnp.concatenate([own, jnp.zeros((5, 256), F32)], axis=0).T
        for axis in range(3):
            wide = jnp.broadcast_to(own[:, axis : axis + 1], (256, 128))
            wide_ref[leaf, axis] = wide.reshape(32, 8, 128)

    def leaf_step(leaf, carry):
        total = jnp.zeros((8, 256), F32)
        for slot in range(8):
            sides, halves = source_of(base_leaf + leaf, slot)
            bands = []
            for band in range(0, 32, 8):
                tiles = []
                target = [wide_ref[leaf, axis, band : band + 8] for axis in range(3)]
                for place in halves:
                    first = target[0] - place[0]
                    second = target[1] - place[1]
                    third = target[2] - place[2]
                    dist_sq = first * first + second * second + third * third
                    inverse = lax.rsqrt(dist_sq * scale + floor)
                    tiles.append(inverse.reshape(64, 128).astype(BF16))
                bands.append(jnp.concatenate(tiles, axis=1))
            tile = jnp.concatenate(bands, axis=0)
            total += lax.dot_general(sides, tile, NT, preferred_element_type=F32)
        near_ref[leaf] = total
        return carry

    lax.fori_loop(0, 2, leaf_step, 0, unroll=2)


def couple(matrices, sources):
    slots = matrices.shape[0]
    products = lax.dot_general(
        matrices.reshape(slots * 64, 64), sources.astype(BF16), NT, preferred_element_type=F32
    )
    group = lax.broadcasted_iota(jnp.int32, (64, 128), 1) // 8
    total = products[:64]
    for slot in range(1, slots):
        total = jnp.where(group == slot, products[slot * 64 : slot * 64 + 64], total)
    return total


def sum_groups(total):
    for shift in (64, 32, 16, 8):
        total = total + pltpu.roll(total, shift, 1)
    return total


def far_kernel(
    groups,
    cols,
    zs,
    coupling_list_ref,
    coupling_count_ref,
    coarse_list_ref,
    coarse_count_ref,
    owner_ref,
    coeffs_ref,
    last_ref,
    last_mate_ref,
    beyond_ref,
    leaf_coupling_ref,
    coarse_coupling_ref,
    transfer_ref,
    basis_ref,
    near_low_ref,
    near_high_ref,
    out_ref,
    source_ref,
):
    my_core = lax.axis_index("core")
    for slot in range(16):
        device = owner_ref[coarse_list_ref[0, slot]]
        row = lax.shift_right_logical(device, cols.bit_length() - 1)
        col = device & (cols - 1)
        z = col & (zs - 1)
        order = jnp.where(z < zs // 2, z * 2, (zs - z) * 2 + 1)
        order = jnp.where(z == 0, 1, jnp.where(z == zs // 2, 0, order))
        tile_id = (row >> 1) * (cols // 4) + ((col - z + order) >> 2)
        mine = (row & 1) == my_core
        tile = jnp.where(mine, last_ref[tile_id], last_mate_ref[tile_id]).astype(F32)
        place = order & 3
        picked = tile[0:4]
        for step in range(1, 4):
            picked = jnp.where(place == step, tile[step * 4 : step * 4 + 4], picked)
        picked = jnp.where(slot < coarse_count_ref[0], picked, 0.0)
        source_ref[4, slot * 8 : slot * 8 + 8, :] = jnp.concatenate(
            [picked[:, :64], picked[:, 64:]], axis=0
        )
    for leaf in range(4):
        for slot in range(16):
            chip_gap, row, gap, source = locate(coupling_list_ref[leaf, slot], cols)
            far = jnp.abs(gap)
            place = jnp.where(far == 1, 1 + row, 1 + row * 2 + far) + jnp.where(gap < 0, 7, 0)
            place = jnp.where(far == 0, row * 7, place)
            fetched_here = (chip_gap < 0) == (my_core == 0)
            tile = jnp.where(fetched_here, last_ref[groups + place], last_mate_ref[groups + place])
            tile = jnp.where(jnp.abs(chip_gap) == 2, beyond_ref[place], tile)
            tile = jnp.where(chip_gap == 0, coeffs_ref[place], tile).astype(F32)
            half = jnp.where(source >= 2, tile[8:], tile[:8])
            half = jnp.where(source & 1 == 1, half[:, 64:], half[:, :64])
            live = slot < coupling_count_ref[leaf]
            source_ref[leaf, slot * 8 : slot * 8 + 8, :] = jnp.where(live, half, 0.0)
    totals = [couple(leaf_coupling_ref[leaf], source_ref[leaf]) for leaf in range(4)]
    coarse_field = sum_groups(couple(coarse_coupling_ref[0], source_ref[4]))
    field_hi = coarse_field.astype(BF16).astype(F32)
    rest = coarse_field - field_hi
    field_mid = rest.astype(BF16).astype(F32)
    group = lax.broadcasted_iota(jnp.int32, (64, 128), 1) // 8
    parts = jnp.where(group == 2, rest - field_mid, 0.0)
    parts = jnp.where(group == 1, field_mid, jnp.where(group == 0, field_hi, parts)).astype(BF16)
    for leaf in range(4):
        totals[leaf] += jnp.dot(transfer_ref[leaf], parts, preferred_element_type=F32)
    local = sum_groups(jnp.concatenate(totals, axis=0)).T[:8]
    for leaf in range(4):
        mine = local[:, leaf * 64 : leaf * 64 + 64].astype(BF16)
        far_part = lax.dot_general(mine, basis_ref[leaf], NN, preferred_element_type=F32)
        span = slice(leaf * 256, leaf * 256 + 256)
        near_part = near_low_ref[leaf] if leaf < 2 else near_high_ref[leaf - 2]
        out_ref[:, span] = (near_part + far_part).astype(BF16)


VMEM = pl.BlockSpec(memory_space=pltpu.VMEM)
ANY = pl.BlockSpec(memory_space=pl.ANY)
SMEM = pl.BlockSpec(memory_space=pltpu.SMEM)
PARAMS = pltpu.CompilerParams(vmem_limit_bytes=16 * 2**20)


def near_call(base_leaf, cols, *operands):
    return pl.pallas_call(
        functools.partial(near_kernel, base_leaf, cols),
        out_shape=jax.ShapeDtypeStruct((2, 8, 256), F32),
        in_specs=[SMEM] * 2 + [VMEM] * 3,
        out_specs=VMEM,
        scratch_shapes=[pltpu.VMEM((2, 3, 32, 8, 128), F32)],
        compiler_params=PARAMS,
        name=f"near{base_leaf}",
        cost_estimate=pl.CostEstimate(
            flops=100_000_000, bytes_accessed=1_200_000, transcendentals=0
        ),
    )(*operands)


def far_call(groups, cols, zs, *operands):
    return pl.pallas_call(
        functools.partial(far_kernel, groups, cols, zs),
        out_shape=jax.ShapeDtypeStruct((8, 1024), BF16),
        in_specs=[SMEM] * 5 + [VMEM] * 10,
        out_specs=VMEM,
        scratch_shapes=[pltpu.VMEM((5, 128, 64), F32)],
        compiler_params=PARAMS,
        name="far",
    )(*operands)


def per_device(
    xs,
    ys,
    zs,
    rhs,
    points,
    basis,
    transfer,
    leaf_coupling,
    coupling_list,
    coupling_count,
    coarse_coupling,
    coarse_list,
    coarse_count,
    owner,
    near_list,
    near_count,
):
    cols = ys * zs
    groups = xs * cols // 4
    half = zs // 2
    turned = [half, 0] + [z for near in range(1, half) for z in (near, zs - near)]
    basis = jnp.swapaxes(basis, 1, 2)

    blocks, cluster = pl.pallas_call(
        pack_kernel,
        out_shape=(
            jax.ShapeDtypeStruct((2, BLOCK, 16, 128), BF16),
            jax.ShapeDtypeStruct((zs, 4, 128), BF16),
        ),
        in_specs=[VMEM] + [ANY] * 3,
        out_specs=(VMEM, VMEM),
        scratch_shapes=[
            pltpu.VMEM(points.shape, F32),
            pltpu.VMEM(basis.shape, BF16),
            pltpu.VMEM(transfer.shape, BF16),
            pltpu.SemaphoreType.DMA((3,)),
        ],
        name="pack",
    )(rhs, points, basis, transfer)

    def along_col(step):
        pairs = []
        for core in range(2):
            for col in range(cols):
                source = col + step if core == 0 else col - step
                if 0 <= source < cols:
                    pairs.append((core * cols + source, core * cols + col))
        return pairs

    def along_x(step):
        pairs = []
        for x in range(xs):
            for core in range(2):
                source = x - step if core == 0 else x + step
                if 0 <= source < xs:
                    pairs.append((source * 2 + core, x * 2 + core))
        return pairs

    def coeffs_of(window):
        parts = [window[:, place : place + 1] for place in (9, 19, 29)]
        return jnp.concatenate(parts + [window[:, 30:]], axis=1).reshape(14, 16, 128)

    chip = lax.all_gather(blocks, "core", axis=0, tiled=False)
    first = lax.ppermute(chip, ("core", "y", "z"), along_col(1))[:, 0]
    chip, cluster = lax.optimization_barrier((chip, cluster))
    line = lax.all_to_all(
        cluster, "z", 0, 0, tiled=True, axis_index_groups=[turned]
    ).reshape(zs // 4, 16, 128)
    second = jnp.concatenate([chip[:, 0, 9:], first[:, 9:]], axis=1)
    second = lax.ppermute(second, ("core", "y", "z"), along_col(2))
    first, line = lax.optimization_barrier((first, line))
    line = jnp.broadcast_to(line[None], (xs * ys,) + line.shape)
    same = lax.all_to_all(line, ("x", "y"), 0, 0, tiled=True).reshape(groups, 16, 128)

    window = jnp.concatenate(
        [blocks[0], first.reshape(2 * BLOCK, 16, 128), second.reshape(4, 16, 128)], axis=0
    )
    window = lax.all_gather(window, "core", axis=0, tiled=False)
    beside = lax.ppermute(window, ("x", "core"), along_x(1))
    coeffs = coeffs_of(window)
    beyond = lax.ppermute(coeffs, ("x", "core"), along_x(2))
    near_low = near_call(0, cols, near_list, near_count, points, window, beside)
    same, beside, beyond, near_low = lax.optimization_barrier((same, beside, beyond, near_low))
    last = jnp.concatenate([same, coeffs_of(beside)], axis=0)
    last, beside = lax.optimization_barrier((last, beside))
    near_high = near_call(2, cols, near_list, near_count, points, window, beside)
    last_mate = lax.ppermute(last, "core", [(0, 1), (1, 0)])

    return far_call(
        groups,
        cols,
        zs,
        coupling_list,
        coupling_count,
        coarse_list,
        coarse_count,
        owner,
        coeffs,
        last,
        last_mate,
        beyond,
        leaf_coupling,
        coarse_coupling,
        transfer,
        basis,
        near_low,
        near_high,
    )


def solution(mesh):
    rows, cols = mesh.devices.shape
    xs, ys = rows // 2, 4
    zs = cols // ys
    axes = ("x", "core", "y", "z")
    fine = Mesh(mesh.devices.reshape(xs, 2, ys, zs), axes)
    in_specs = (
        P(None, axes),
        P(None, axes),
        P(axes, None, None),
        P(axes, None, None),
        P(axes, None, None, None),
        P(axes, None),
        P(axes),
        P(axes, None, None, None),
        P(axes, None),
        P(axes),
        P(),
        P(axes, None),
        P(axes),
    )
    return jax.shard_map(
        functools.partial(per_device, xs, ys, zs),
        mesh=fine,
        in_specs=in_specs,
        out_specs=P(None, axes),
        check_vma=False,
    )
```
